256 devices in a mesh: img: 32 (over z, x), feat: 8 (over y, core).
Axes of the slice: x: 4, y: 4, z: 8, core: 2. Of those that a mesh axis runs over, the one named last changes fastest.
Arguments:
- view_a: bfloat16 [4096, 2048], P('img'), may hold values from -200 to 200
- view_b: bfloat16 [4096, 2048], P('img'), may hold values from -200 to 200
- projection: bfloat16 [2048, 8192], P(None, 'feat'), may hold values from -2 to 2
Outputs:
- loss: float32 [], replicated
- grad_a: bfloat16 [4096, 2048], P('img', 'feat')
- grad_b: bfloat16 [4096, 2048], P('img', 'feat')
The draws below stay inside these ranges and needn't reach their ends.
All inputs are finite; a program needn't handle non-finite values.
Results may differ from the reference program's by a relative error of at most 0.018.
Values may be sent and summed in bfloat16 or wider, within the bound.
A program may use at most 128 MiB of HBM per device.

```python
import math
import jax
import jax.numpy as jnp
from jax import lax

D = 2048
F = 8192
IMAGES = 4096
N_FEAT = 8


def make_views(key):
    keys = jax.random.split(jax.random.fold_in(key, 17), 5)
    base = jnp.clip(jax.random.normal(keys[0], (IMAGES, D), jnp.float32), -5.0, 5.0)
    noise = jnp.clip(jax.random.normal(keys[1], (IMAGES, D), jnp.float32), -5.0, 5.0)
    rho = jax.random.uniform(keys[2], (IMAGES, 1), jnp.float32, 0.8, 0.95)
    ramp = jnp.exp(math.log(3.0) * jnp.arange(IMAGES, dtype=jnp.float32)[:, None] / max(IMAGES - 1, 1))
    row_scale = jnp.exp(jax.random.uniform(keys[3], (IMAGES, 1), jnp.float32, 0.0, math.log(10.0)))
    col_scale = jnp.exp(jax.random.uniform(keys[4], (1, D), jnp.float32, math.log(0.5), math.log(2.0)))
    scale = 0.3 * ramp * row_scale * col_scale
    first = base * scale
    second = (rho * base + jnp.sqrt(1.0 - rho * rho) * noise) * scale
    return (first, second)


def draw_view_a(key, part):
    return make_views(key)[0].astype(jnp.bfloat16)


def draw_view_b(key, part):
    return make_views(key)[1].astype(jnp.bfloat16)


def draw_projection(key, part):
    keys = jax.random.split(jax.random.fold_in(key, 29), 4)
    width = F // N_FEAT
    common = jnp.clip(jax.random.normal(keys[0], (D, width), jnp.float32), -5.0, 5.0)
    single = jnp.clip(jax.random.normal(keys[1], (D, F), jnp.float32), -5.0, 5.0)
    mixing = jax.random.uniform(keys[2], (1, F), jnp.float32, 0.75, 0.98)
    signs = (2 * jax.random.randint(keys[3], (1, F), 0, 2) - 1).astype(jnp.float32)
    tiled = jnp.tile(common, (1, N_FEAT))
    weight = (mixing * signs * tiled + jnp.sqrt(1.0 - mixing * mixing) * single) / math.sqrt(D)
    return weight.astype(jnp.bfloat16)


def setup_inputs(seed: int = 0) -> dict:
    arg_keys = jax.random.split(jax.random.key(seed), 4)
    return {
        "view_a": draw_view_a(jax.random.fold_in(arg_keys[3], 71), 0),
        "view_b": draw_view_b(jax.random.fold_in(arg_keys[3], 71), 0),
        "projection": draw_projection(jax.random.fold_in(arg_keys[3], 71), 0),
    }


LAMBDA = 0.0051
EPSILON = 1e-05

def standardize(values):
    mean_ab = lax.optimization_barrier(jnp.mean(values, axis=0))
    centered = values - mean_ab
    variance = lax.optimization_barrier(jnp.mean(centered * centered, axis=0))
    rstd_ab = lax.rsqrt(variance + EPSILON)
    return (centered * rstd_ab, rstd_ab)

def back_standard(grad, hat_ab, rstd_ab):
    first = lax.optimization_barrier(jnp.mean(grad, axis=0))
    second = lax.optimization_barrier(jnp.mean(grad * hat_ab, axis=0))
    return rstd_ab * (grad - first - hat_ab * second)

def reference(view_a, view_b, projection):
    images = view_a.shape[0]
    proj_a = jnp.dot(view_a, projection, preferred_element_type=jnp.float32)
    proj_b = jnp.dot(view_b, projection, preferred_element_type=jnp.float32)
    hat_a, rstd_a = standardize(proj_a)
    hat_b, rstd_b = standardize(proj_b)
    norm_a = hat_a.astype(jnp.bfloat16)
    norm_b = hat_b.astype(jnp.bfloat16)
    wide_a = norm_a.astype(jnp.float32)
    wide_b = norm_b.astype(jnp.float32)
    corr = lax.optimization_barrier(jnp.sum(wide_a * wide_b, axis=0)) / images
    gram_a = jnp.dot(norm_a, norm_a.T, preferred_element_type=jnp.float32)
    gram_b = jnp.dot(norm_b, norm_b.T, preferred_element_type=jnp.float32)
    frobenius = jnp.sum(gram_a * gram_b)
    loss = jnp.sum((1.0 - corr) ** 2) - LAMBDA * jnp.sum(corr * corr) + LAMBDA * frobenius / (images * images)
    factor = -2.0 * (1.0 - corr) - 2.0 * LAMBDA * corr
    coef = 2.0 * LAMBDA / images
    grad_na = coef * jnp.dot(gram_b.astype(jnp.bfloat16), norm_a, preferred_element_type=jnp.float32) + wide_b * factor
    grad_nb = coef * jnp.dot(gram_a.astype(jnp.bfloat16), norm_b, preferred_element_type=jnp.float32) + wide_a * factor
    grad_pa = back_standard(grad_na, hat_a, rstd_a).astype(jnp.bfloat16)
    grad_pb = back_standard(grad_nb, hat_b, rstd_b).astype(jnp.bfloat16)
    grad_a = jnp.dot(grad_pa, projection.T, preferred_element_type=jnp.float32).astype(jnp.bfloat16)
    grad_b = jnp.dot(grad_pb, projection.T, preferred_element_type=jnp.float32).astype(jnp.bfloat16)
    return (loss, grad_a, grad_b)
```

```python
import functools
import jax
import jax.numpy as jnp
from jax import lax
from jax.experimental import pallas as pl
from jax.experimental.pallas import tpu as pltpu
from jax.sharding import PartitionSpec as P

LAMBDA = 0.0051
EPSILON = 1e-05
MESH = pl.DeviceIdType.MESH
NZ, NX, NY = 8, 4, 4
F32, BF16 = jnp.float32, jnp.bfloat16
NEAR_Z = (1, 7, 2, 6, 3, 5, 4)
NEAR_4 = (1, 3, 2)


def remote(src, dst, send_sem, recv_sem, device):
    return pltpu.make_async_remote_copy(
        src_ref=src, dst_ref=dst, send_sem=send_sem, recv_sem=recv_sem,
        device_id=device, device_id_type=MESH,
    )


def dot_nt(a, b):
    return lax.dot_general(a, b, (((1,), (1,)), ((), ())), preferred_element_type=F32)


def dot_nn(a, b):
    return jnp.dot(a, b, preferred_element_type=F32)


def merge(parts, count):
    n = len(parts)
    ma = sum(p[0] for p in parts) * (1.0 / n)
    mb = sum(p[1] for p in parts) * (1.0 / n)
    da = [p[0] - ma for p in parts]
    db = [p[1] - mb for p in parts]
    saa = sum(p[2] for p in parts) + count * sum(d * d for d in da)
    sbb = sum(p[3] for p in parts) + count * sum(d * d for d in db)
    sab = sum(p[4] for p in parts) + count * sum(d * e for d, e in zip(da, db))
    return [ma, mb, saa, sbb, sab]


def kernel(
    va, vb, proj, loss_ref, ga_ref, gb_ref,
    vv, pw, hat, hr, grad, back,
    tp, txr, txs, tzr, tfull, mxl, mxr, mzs, mzr, mcorr,
    stx, stz, lcs, lcr, lys, lyr, la, lb,
    zcs, zcr, zys, zyr, zall, gsx, gsz,
    ocs, ocr, oys, oyr, lo, lorc, lo2, lory,
    in_sem, tx_s, tx_r, mx_s, mx_r, tz_s, tz_r, mz_s, mz_r, az_s, az_r, ax_s, ax_r,
    sx_s, sx_r, sz_s, sz_r, lc_s, lc_r, ly_s, ly_r, lay_s, lay_r, lac_s, lac_r,
    zc_s, zc_r, zy_s, zy_r, zay_s, zay_r, zac_s, zac_r, zby_s, zby_r, zbc_s, zbc_r,
    gx_s, gx_r, gz_s, gz_r, oc_s, oc_r, oy_s, oy_r, lo_s, lo_r,
):
    images = 128 * NZ * NX
    img, feat = lax.axis_index("img"), lax.axis_index("feat")
    z, x = lax.div(img, NX), lax.rem(img, NX)
    y, core = lax.div(feat, 2), lax.rem(feat, 2)
    zs = [lax.rem(z + d, NZ) for d in range(NZ)]
    xs = [lax.rem(x + d, NX) for d in range(NX)]
    ys = [lax.rem(y + d, NY) for d in range(NY)]
    yback = [lax.rem(y + NY - d, NY) for d in range(NY)]
    zback = [lax.rem(z + NZ - d, NZ) for d in range(NZ)]
    zdev = [(v * NX + x, feat) for v in zs]
    xdev = [(z * NX + v, feat) for v in xs]
    ydev = [(img, v * 2 + core) for v in ys]
    cdev = (img, y * 2 + 1 - core)

    loads = [
        pltpu.make_async_copy(va, vv.at[pl.ds(0, 128)], in_sem.at[0]),
        pltpu.make_async_copy(vb, vv.at[pl.ds(128, 128)], in_sem.at[1]),
        pltpu.make_async_copy(proj, pw, in_sem.at[2]),
    ]
    for cp in loads:
        cp.start()
    barrier = pltpu.get_barrier_semaphore()
    peers = zdev[1:] + xdev[1:] + ydev[1:] + [cdev]
    for peer in peers:
        pl.semaphore_signal(barrier, inc=1, device_id=peer, device_id_type=MESH)

    sent = []

    def send(src, dst, send_sem, recv_sem, device):
        cp = remote(src, dst, send_sem, recv_sem, device)
        cp.start()
        sent.append(cp)
        return cp

    loads[0].wait()
    loads[1].wait()
    bcols = vv[128:256, pl.ds(pl.multiple_of(feat * 256, 256), 256)].astype(F32)
    bmean = jnp.sum(bcols, axis=0, keepdims=True) * (1.0 / 128)
    ct = (bcols - bmean).T.astype(BF16)
    mxl[8:9, :] = bmean
    for i in range(8):
        acols = vv[0:128, i * 256:(i + 1) * 256].astype(F32)
        amean = jnp.sum(acols, axis=0, keepdims=True) * (1.0 / 128)
        mxl[i:i + 1, :] = amean
        tp[i] = dot_nn(ct, (acols - amean).astype(BF16)).astype(BF16)
    pl.semaphore_wait(barrier, len(peers))
    mx, tx = {}, {}
    for d in NEAR_4:
        mx[d] = send(mxl, mxr.at[d - 1], mx_s.at[d - 1], mx_r.at[d - 1], xdev[d])
    for d in NEAR_4:
        tx[d] = send(
            tp.at[:, pl.ds(pl.multiple_of(xs[d] * 64, 64), 64), :], txr.at[d - 1],
            tx_s.at[d - 1], tx_r.at[d - 1], xdev[d],
        )

    loads[2].wait()

    def project(n, carry):
        cols = pl.ds(pl.multiple_of(n * 256, 256), 256)
        pr = dot_nn(vv[...], pw[:, cols])
        hat[:, cols] = pr
        pa, pb = pr[0:128], pr[128:256]
        ma = jnp.sum(pa, axis=0, keepdims=True) * (1.0 / 128)
        mb = jnp.sum(pb, axis=0, keepdims=True) * (1.0 / 128)
        pa, pb = pa - ma, pb - mb
        stx[x, 0, :, cols] = ma
        stx[x, 1, :, cols] = mb
        stx[x, 2, :, cols] = jnp.sum(pa * pa, axis=0, keepdims=True)
        stx[x, 3, :, cols] = jnp.sum(pb * pb, axis=0, keepdims=True)
        stx[x, 4, :, cols] = jnp.sum(pa * pb, axis=0, keepdims=True)
        return carry

    lax.fori_loop(0, 4, project, 0)
    sx = {d: send(stx.at[x], stx.at[x], sx_s.at[d - 1], sx_r.at[d - 1], xdev[d]) for d in NEAR_4}
    for d in NEAR_4:
        sx[d].wait_recv()
    merged = merge([[stx[k, i] for i in range(5)] for k in range(NX)], 128.0)
    for i in range(5):
        stz[z, i] = merged[i]
    sz = {d: send(stz.at[z], stz.at[z], sz_s.at[d - 1], sz_r.at[d - 1], zdev[d]) for d in NEAR_Z}

    for d in NEAR_4:
        mx[d].wait_recv()
    for i in range(8):
        for r in range(4):
            am = mxl[i:i + 1, :] if r == 0 else mxr[r - 1, i:i + 1, :]
            bm = mxl[8:9, :] if r == 0 else mxr[r - 1, 8:9, :]
            mzs[i, 0, r:r + 1, :] = am
            mzs[i, 0, r + 4:r + 5, :] = am
            mzs[i, 1, r:r + 1, :] = bm
            mzs[i, 1, r + 4:r + 5, :] = bm
    mz, tz = {}, {}
    for d in NEAR_Z:
        mz[d] = send(mzs.at[zs[d]], mzr.at[d - 1], mz_s.at[d - 1], mz_r.at[d - 1], zdev[d])
    xrows = pl.ds(pl.multiple_of(x * 64, 64), 64)

    def z_scatter():
        for d in NEAR_4:
            tx[d].wait_recv()
        for i in range(8):
            total = tp[i, xrows, :].astype(F32)
            for k in range(3):
                total = total + txr[k, i].astype(F32)
            txs[i] = total.astype(BF16)
        for d in NEAR_Z:
            tz[d] = send(txs.at[zs[d]], tzr.at[d - 1], tz_s.at[d - 1], tz_r.at[d - 1], zdev[d])

    for d in NEAR_Z:
        sz[d].wait_recv()
    mean_a, mean_b, saa, sbb, sab = merge(
        [[stz[k, i] for i in range(5)] for k in range(NZ)], 128.0 * NX
    )
    rstd_a = lax.rsqrt(saa * (1.0 / images) + EPSILON)
    rstd_b = lax.rsqrt(sbb * (1.0 / images) + EPSILON)
    corr = sab * rstd_a * rstd_b * (1.0 / images)
    factor = -2.0 * (1.0 - corr) - 2.0 * LAMBDA * corr
    coef = 2.0 * LAMBDA / images
    diag = jnp.sum((1.0 - corr) ** 2 - LAMBDA * corr * corr, axis=1, keepdims=True)
    hat_a = (hat[0:128, :] - mean_a) * rstd_a
    hat[0:128, :] = hat_a
    hr[0:128, :] = (hat_a * rstd_a).astype(BF16)
    hat_b = (hat[128:256, :] - mean_b) * rstd_b
    hat[128:256, :] = hat_b
    hr[128:256, :] = (hat_b * rstd_b).astype(BF16)

    def feat_scatter(chunk, cs, cr, y_send, y_recv, cs_s, cs_r, ysem_s, ysem_r):
        cc, yc = {}, {}
        for d in (1, 3, 2, 0):
            cs[d] = chunk(ys[d] * 2 + 1 - core).astype(BF16)
            cc[d] = send(cs.at[d], cr.at[d], cs_s.at[d], cs_r.at[d], cdev)
        for d in NEAR_4:
            own = chunk(ys[d] * 2 + core)
            cc[d].wait_recv()
            y_send[d - 1] = (own + cr[d].astype(F32)).astype(BF16)
            yc[d] = send(y_send.at[d - 1], y_recv.at[d - 1], ysem_s.at[d - 1], ysem_r.at[d - 1], ydev[d])
        total = chunk(feat)
        cc[0].wait_recv()
        total = total + cr[0].astype(F32)

        def finish():
            out = total
            for d in NEAR_4:
                yc[d].wait_recv()
                out = out + y_recv[d - 1].astype(F32)
            return out

        return finish

    def feat_gather(at, y_s, y_r, c_s, c_r):
        yc = {d: send(at(feat), at(feat), y_s.at[d - 1], y_r.at[d - 1], ydev[d]) for d in NEAR_4}
        cc = {0: send(at(feat), at(feat), c_s.at[0], c_r.at[0], cdev)}

        def forward():
            for d in NEAR_4:
                yc[d].wait_recv()
                there = at(yback[d] * 2 + core)
                cc[d] = send(there, there, c_s.at[d], c_r.at[d], cdev)

        def finish():
            for d in range(4):
                cc[d].wait_recv()

        return forward, finish

    def rows_of_p(i):
        return pw[pl.ds(pl.multiple_of(i * 256, 256), 256), :]

    l_finish = feat_scatter(
        lambda i: dot_nt(hr[...], rows_of_p(i)), lcs, lcr, lys, lyr, lc_s, lc_r, ly_s, ly_r
    )
    z_scatter()

    total = l_finish()
    la[feat] = total[0:128].astype(BF16)
    lb[...] = total[128:256].astype(BF16)
    la_forward, la_finish = feat_gather(lambda i: la.at[i], lay_s, lay_r, lac_s, lac_r)
    for d in NEAR_Z:
        mz[d].wait_recv()
    am = jnp.concatenate([mzs[z, 0]] + [mzr[k, 0] for k in range(7)], axis=0)
    bm = jnp.concatenate([mzs[z, 1]] + [mzr[k, 1] for k in range(7)], axis=0)
    am = am - jnp.sum(am, axis=0, keepdims=True) * (1.0 / 64)
    bm = bm - jnp.sum(bm, axis=0, keepdims=True) * (1.0 / 64)
    mcorr[...] = dot_nn((bm * 64.0).T.astype(BF16), am.astype(BF16))
    total = txs[z].astype(F32) + mcorr[xrows, :]
    for d in NEAR_Z:
        tz[d].wait_recv()
        total = total + tzr[d - 1].astype(F32)
    tfull[z, xrows, :] = total.astype(BF16)
    mine = tfull.at[z, xrows, :]
    az = {d: send(mine, mine, az_s.at[d - 1], az_r.at[d - 1], zdev[d]) for d in NEAR_Z}
    ax = {}
    for e in NEAR_4:
        ax[0, e] = send(mine, mine, ax_s.at[0, e - 1], ax_r.at[0, e - 1], xdev[e])
    la_forward()
    for d in NEAR_Z:
        az[d].wait_recv()
        there = tfull.at[zback[d], xrows, :]
        for e in NEAR_4:
            ax[d, e] = send(there, there, ax_s.at[d, e - 1], ax_r.at[d, e - 1], xdev[e])
    la_finish()
    for d in (0,) + NEAR_Z:
        for e in NEAR_4:
            ax[d, e].wait_recv()

    za_finish = feat_scatter(
        lambda i: dot_nn(lb[...], tfull[i]), zcs, zcr, zys, zyr, zc_s, zc_r, zy_s, zy_r
    )
    zb = sum(dot_nt(la[i], tfull[i]) for i in range(8))
    zall[feat, 128:256, :] = zb.astype(BF16)
    zb_forward, zb_finish = feat_gather(
        lambda i: zall.at[i, pl.ds(128, 128), :], zby_s, zby_r, zbc_s, zbc_r
    )
    zall[feat, 0:128, :] = za_finish().astype(BF16)
    za_forward, za_finish2 = feat_gather(
        lambda i: zall.at[i, pl.ds(0, 128), :], zay_s, zay_r, zac_s, zac_r
    )
    zb_forward()
    za_forward()
    zb_finish()
    za_finish2()

    back[0] = rstd_a
    back[1] = rstd_b
    back[2] = factor

    def gradient(n, carry):
        cols = pl.ds(pl.multiple_of(n * 256, 256), 256)
        g = sum(dot_nn(zall[i], pw[i * 256:(i + 1) * 256, cols]) for i in range(8))
        ra, rb, fac = back[0, :, cols], back[1, :, cols], back[2, :, cols]
        ha, hb = hat[0:128, cols], hat[128:256, cols]
        qa = g[0:128] * ra
        na = coef * qa + hb * fac
        nb = coef * (g[128:256] * rb) + ha * fac
        grad[0:128, cols] = na
        grad[128:256, cols] = nb
        gsx[x, 0, :, cols] = jnp.sum(na, axis=0, keepdims=True)
        gsx[x, 1, :, cols] = jnp.sum(nb, axis=0, keepdims=True)
        gsx[x, 2, :, cols] = jnp.sum(na * ha, axis=0, keepdims=True)
        gsx[x, 3, :, cols] = jnp.sum(nb * hb, axis=0, keepdims=True)
        gsx[x, 4, :, cols] = jnp.sum(qa * ha, axis=0, keepdims=True)
        return carry

    lax.fori_loop(0, 4, gradient, 0)
    gx = {d: send(gsx.at[x], gsx.at[x], gx_s.at[d - 1], gx_r.at[d - 1], xdev[d]) for d in NEAR_4}
    for d in NEAR_4:
        gx[d].wait_recv()
    for i in range(5):
        gsz[z, i] = (gsx[0, i] + gsx[1, i]) + (gsx[2, i] + gsx[3, i])
    gz = {d: send(gsz.at[z], gsz.at[z], gz_s.at[d - 1], gz_r.at[d - 1], zdev[d]) for d in NEAR_Z}
    for d in NEAR_Z:
        gz[d].wait_recv()
    sums = [sum(gsz[k, i] for k in range(NZ)) for i in range(5)]
    means = [s * (1.0 / images) for s in sums[:4]]
    hr[0:128, :] = (rstd_a * (grad[0:128, :] - means[0] - hat[0:128, :] * means[2])).astype(BF16)
    hr[128:256, :] = (rstd_b * (grad[128:256, :] - means[1] - hat[128:256, :] * means[3])).astype(BF16)

    share = diag + (LAMBDA / (images * images)) * jnp.sum(sums[4], axis=1, keepdims=True)
    lo[...] = jnp.broadcast_to(share, (8, 128))
    lc = send(lo, lorc, lo_s.at[0], lo_r.at[0], cdev)
    o_finish = feat_scatter(
        lambda i: dot_nt(hr[...], rows_of_p(i)), ocs, ocr, oys, oyr, oc_s, oc_r, oy_s, oy_r
    )
    lc.wait_recv()
    pair = jnp.where(core == 0, lo[...] + lorc[...], lorc[...] + lo[...])
    lo2[...] = pair
    lly = {d: send(lo2, lory.at[y], lo_s.at[d], lo_r.at[d], ydev[d]) for d in NEAR_4}
    lory[y] = pair
    total = o_finish()
    ga_ref[...] = total[0:128].astype(BF16)
    gb_ref[...] = total[128:256].astype(BF16)
    for d in NEAR_4:
        lly[d].wait_recv()
    loss_ref[...] = (lory[0] + lory[1]) + (lory[2] + lory[3])
    for cp in sent:
        cp.wait_send()


def on_device(view_a, view_b, projection):
    dma = pltpu.SemaphoreType.DMA
    vmem = pltpu.VMEM
    scratch = [
        vmem((256, 2048), BF16), vmem((2048, 1024), BF16), vmem((256, 1024), F32),
        vmem((256, 1024), BF16), vmem((256, 1024), F32), vmem((3, 1, 1024), F32),
        vmem((8, 256, 256), BF16), vmem((3, 8, 64, 256), BF16), vmem((8, 64, 256), BF16),
        vmem((7, 64, 256), BF16), vmem((8, 256, 256), BF16),
        vmem((16, 256), F32), vmem((3, 16, 256), F32),
        vmem((8, 2, 8, 256), F32), vmem((7, 2, 8, 256), F32), vmem((256, 256), F32),
        vmem((4, 5, 1, 1024), F32), vmem((8, 5, 1, 1024), F32),
        vmem((4, 256, 256), BF16), vmem((4, 256, 256), BF16), vmem((3, 256, 256), BF16),
        vmem((3, 256, 256), BF16), vmem((8, 128, 256), BF16), vmem((128, 256), BF16),
        vmem((4, 128, 256), BF16), vmem((4, 128, 256), BF16), vmem((3, 128, 256), BF16),
        vmem((3, 128, 256), BF16), vmem((8, 256, 256), BF16),
        vmem((4, 5, 1, 1024), F32), vmem((8, 5, 1, 1024), F32),
        vmem((4, 256, 256), BF16), vmem((4, 256, 256), BF16), vmem((3, 256, 256), BF16),
        vmem((3, 256, 256), BF16),
        vmem((8, 128), F32), vmem((8, 128), F32), vmem((8, 128), F32), vmem((4, 8, 128), F32),
        dma((3,)),
    ]
    sizes = [
        (3,), (3,), (7,), (7,), (7,), (8, 3),
        (3,), (7,), (4,), (3,), (3,), (4,),
        (4,), (3,), (3,), (4,), (3,), (4,),
        (3,), (7,), (4,), (3,), (4,),
    ]
    for s in sizes:
        scratch += [dma(s), dma(s)]
    loss, ga, gb = pl.pallas_call(
        kernel,
        out_shape=(
            jax.ShapeDtypeStruct((8, 128), F32),
            jax.ShapeDtypeStruct((128, 256), BF16),
            jax.ShapeDtypeStruct((128, 256), BF16),
        ),
        in_specs=[pl.BlockSpec(memory_space=pl.ANY)] * 3,
        out_specs=[pl.BlockSpec(memory_space=pltpu.VMEM)] * 3,
        scratch_shapes=scratch,
        compiler_params=pltpu.CompilerParams(
            collective_id=0, has_side_effects=True, vmem_limit_bytes=48 * 1024 * 1024
        ),
        cost_estimate=pl.CostEstimate(flops=5 * 10**9, bytes_accessed=6 * 10**6, transcendentals=0),
        name="twins",
    )(view_a, view_b, projection)
    return loss[0, 0], ga, gb


def solution(mesh):
    in_specs = (P("img", None), P("img", None), P(None, "feat"))
    out_specs = (P(), P("img", "feat"), P("img", "feat"))
    return jax.shard_map(
        on_device, mesh=mesh, in_specs=in_specs, out_specs=out_specs, check_vma=False
    )
```

```python
import functools
import jax
import jax.numpy as jnp
from jax import lax
from jax.experimental import pallas as pl
from jax.experimental.pallas import tpu as pltpu
from jax.sharding import PartitionSpec as P

LAMBDA = 0.0051
EPSILON = 1e-05
MESH = pl.DeviceIdType.MESH
NZ, NX, NY = 8, 4, 4
F32, BF16 = jnp.float32, jnp.bfloat16
NEAR_Z = (1, 7, 2, 6, 3, 5, 4)
NEAR_4 = (1, 3, 2)


def remote(src, dst, send_sem, recv_sem, device):
    return pltpu.make_async_remote_copy(
        src_ref=src, dst_ref=dst, send_sem=send_sem, recv_sem=recv_sem,
        device_id=device, device_id_type=MESH,
    )


def dot_nt(a, b):
    return lax.dot_general(a, b, (((1,), (1,)), ((), ())), preferred_element_type=F32)


def dot_nn(a, b):
    return jnp.dot(a, b, preferred_element_type=F32)


def merge(parts, count):
    n = len(parts)
    ma = sum(p[0] for p in parts) * (1.0 / n)
    mb = sum(p[1] for p in parts) * (1.0 / n)
    da = [p[0] - ma for p in parts]
    db = [p[1] - mb for p in parts]
    saa = sum(p[2] for p in parts) + count * sum(d * d for d in da)
    sbb = sum(p[3] for p in parts) + count * sum(d * d for d in db)
    sab = sum(p[4] for p in parts) + count * sum(d * e for d, e in zip(da, db))
    return [ma, mb, saa, sbb, sab]


def kernel(
    va, vb, proj, loss_ref, grads_ref,
    vv, pw, hat, hr, grad, back,
    xa, xb, tp, tzr, tfull, mz, mcorr,
    stx, stz, lcs, lcr, lys, lyr, la, lb,
    zcs, zcr, zys, zyr, zall, gsx, gsz,
    ocs, ocr, oys, oyr, lo, lorc, lo2, lory,
    in_sem, xa_s, xa_r, xb_s, xb_r, xc_s, xc_r, tz_s, tz_r, mz_s, mz_r, az_s, az_r, ax_s, ax_r,
    sx_s, sx_r, sz_s, sz_r, lc_s, lc_r, ly_s, ly_r, lay_s, lay_r, lac_s, lac_r,
    zc_s, zc_r, zy_s, zy_r, zay_s, zay_r, zac_s, zac_r, zby_s, zby_r, zbc_s, zbc_r,
    gx_s, gx_r, gz_s, gz_r, oc_s, oc_r, oy_s, oy_r, lo_s, lo_r,
):
    images = 128 * NZ * NX
    img, feat = lax.axis_index("img"), lax.axis_index("feat")
    z, x = lax.div(img, NX), lax.rem(img, NX)
    y, core = lax.div(feat, 2), lax.rem(feat, 2)
    zs = [lax.rem(z + d, NZ) for d in range(NZ)]
    xs = [lax.rem(x + d, NX) for d in range(NX)]
    ys = [lax.rem(y + d, NY) for d in range(NY)]
    xback = [lax.rem(x + NX - d, NX) for d in range(NX)]
    yback = [lax.rem(y + NY - d, NY) for d in range(NY)]
    zback = [lax.rem(z + NZ - d, NZ) for d in range(NZ)]
    zdev = [(v * NX + x, feat) for v in zs]
    xdev = [(z * NX + v, feat) for v in xs]
    ydev = [(img, v * 2 + core) for v in ys]
    cdev = (img, y * 2 + 1 - core)

    loads = [
        pltpu.make_async_copy(va, vv.at[pl.ds(0, 128)], in_sem.at[0]),
        pltpu.make_async_copy(vb, vv.at[pl.ds(128, 128)], in_sem.at[1]),
        pltpu.make_async_copy(proj, pw, in_sem.at[2]),
    ]
    for cp in loads:
        cp.start()
    barrier = pltpu.get_barrier_semaphore()
    peers = zdev[1:] + xdev[1:] + ydev[1:] + [cdev]
    for peer in peers:
        pl.semaphore_signal(barrier, inc=1, device_id=peer, device_id_type=MESH)

    sent = []

    def send(src, dst, send_sem, recv_sem, device):
        cp = remote(src, dst, send_sem, recv_sem, device)
        cp.start()
        sent.append(cp)
        return cp

    def cols256(i):
        return pl.ds(pl.multiple_of(i * 256, 256), 256)

    loads[0].wait()
    loads[1].wait()
    xa[0, x] = vv[0:128, cols256(x * 2)]
    xa[1, x] = vv[0:128, cols256(x * 2 + 1)]
    xb[x] = vv[128:256, cols256(feat)]
    loads[2].wait()

    def project(n, carry):
        cols = pl.ds(pl.multiple_of(n * 256, 256), 256)
        pr = dot_nn(vv[...], pw[:, cols])
        hat[:, cols] = pr
        pa, pb = pr[0:128], pr[128:256]
        ma = jnp.sum(pa, axis=0, keepdims=True) * (1.0 / 128)
        mb = jnp.sum(pb, axis=0, keepdims=True) * (1.0 / 128)
        pa, pb = pa - ma, pb - mb
        stx[x, 0, :, cols] = ma
        stx[x, 1, :, cols] = mb
        stx[x, 2, :, cols] = jnp.sum(pa * pa, axis=0, keepdims=True)
        stx[x, 3, :, cols] = jnp.sum(pb * pb, axis=0, keepdims=True)
        stx[x, 4, :, cols] = jnp.sum(pa * pb, axis=0, keepdims=True)
        return carry

    lax.fori_loop(0, 4, project, 0)
    pl.semaphore_wait(barrier, len(peers))
    sx = {d: send(stx.at[x], stx.at[x], sx_s.at[d - 1], sx_r.at[d - 1], xdev[d]) for d in NEAR_4}

    xac, xbc, xcc = {}, {}, {}
    for d in (2, 1, 3):
        xac[d] = send(
            vv.at[pl.ds(0, 128), cols256(xs[d] * 2 + core)], xa.at[core, x],
            xa_s.at[d - 1], xa_r.at[d - 1], xdev[d],
        )
        xbc[d] = send(
            vv.at[pl.ds(128, 128), cols256(feat)], xb.at[x],
            xb_s.at[d - 1], xb_r.at[d - 1], xdev[d],
        )

    for d in NEAR_4:
        sx[d].wait_recv()
    merged = merge([[stx[k, i] for i in range(5)] for k in range(NX)], 128.0)
    for i in range(5):
        stz[z, i] = merged[i]
    sz = {d: send(stz.at[z], stz.at[z], sz_s.at[d - 1], sz_r.at[d - 1], zdev[d]) for d in NEAR_Z}

    for d in NEAR_4:
        xac[d].wait_recv()
        there = xa.at[core, xback[d]]
        xcc[d] = send(there, there, xc_s.at[d - 1], xc_r.at[d - 1], cdev)

    for d in NEAR_4:
        xbc[d].wait_recv()
    bcols = xb[...].reshape(512, 256).astype(F32)
    bmean = jnp.sum(bcols, axis=0, keepdims=True) * (1.0 / 512)
    ct = (bcols - bmean).T.astype(BF16)
    mz[z, 2] = bmean
    for d in NEAR_4:
        xcc[d].wait_recv()
    for h in range(2):
        acols = xa[h].reshape(512, 256).astype(F32)
        amean = jnp.sum(acols, axis=0, keepdims=True) * (1.0 / 512)
        mz[z, h] = amean
        tp[h] = dot_nn(ct, (acols - amean).astype(BF16)).astype(BF16)
    mzc, tz = {}, {}
    for d in NEAR_Z:
        tz[d] = send(
            tp.at[:, pl.ds(pl.multiple_of(zs[d] * 32, 32), 32), :], tzr.at[d - 1],
            tz_s.at[d - 1], tz_r.at[d - 1], zdev[d],
        )
        mzc[d] = send(mz.at[z], mz.at[z], mz_s.at[d - 1], mz_r.at[d - 1], zdev[d])

    for d in NEAR_Z:
        sz[d].wait_recv()
    mean_a, mean_b, saa, sbb, sab = merge(
        [[stz[k, i] for i in range(5)] for k in range(NZ)], 128.0 * NX
    )
    rstd_a = lax.rsqrt(saa * (1.0 / images) + EPSILON)
    rstd_b = lax.rsqrt(sbb * (1.0 / images) + EPSILON)
    corr = sab * rstd_a * rstd_b * (1.0 / images)
    factor = -2.0 * (1.0 - corr) - 2.0 * LAMBDA * corr
    coef = 2.0 * LAMBDA / images
    diag = jnp.sum((1.0 - corr) ** 2 - LAMBDA * corr * corr, axis=1, keepdims=True)
    hat_a = (hat[0:128, :] - mean_a) * rstd_a
    hat[0:128, :] = hat_a
    hr[0:128, :] = (hat_a * rstd_a).astype(BF16)
    hat_b = (hat[128:256, :] - mean_b) * rstd_b
    hat[128:256, :] = hat_b
    hr[128:256, :] = (hat_b * rstd_b).astype(BF16)

    def feat_scatter(chunk, cs, cr, y_send, y_recv, cs_s, cs_r, ysem_s, ysem_r, between=None):
        cc, yc = {}, {}

        def other(d):
            cs[d] = chunk(ys[d] * 2 + 1 - core).astype(BF16)
            cc[d] = send(cs.at[d], cr.at[d], cs_s.at[d], cs_r.at[d], cdev)

        def own(d):
            mine = chunk(ys[d] * 2 + core)
            cc[d].wait_recv()
            y_send[d - 1] = (mine + cr[d].astype(F32)).astype(BF16)
            yc[d] = send(y_send.at[d - 1], y_recv.at[d - 1], ysem_s.at[d - 1], ysem_r.at[d - 1], ydev[d])

        other(2)
        other(1)
        other(3)
        if between is not None:
            other(0)
            between()
        own(2)
        own(1)
        own(3)
        if between is None:
            other(0)
        total = chunk(feat)
        cc[0].wait_recv()
        total = total + cr[0].astype(F32)

        def finish():
            out = total
            for d in NEAR_4:
                yc[d].wait_recv()
                out = out + y_recv[d - 1].astype(F32)
            return out

        return finish

    def feat_gather(at, y_s, y_r, c_s, c_r):
        yc = {d: send(at(feat), at(feat), y_s.at[d - 1], y_r.at[d - 1], ydev[d]) for d in NEAR_4}
        cc = {0: send(at(feat), at(feat), c_s.at[0], c_r.at[0], cdev)}

        def forward():
            for d in NEAR_4:
                yc[d].wait_recv()
                there = at(yback[d] * 2 + core)
                cc[d] = send(there, there, c_s.at[d], c_r.at[d], cdev)

        def finish():
            for d in range(4):
                cc[d].wait_recv()

        return forward, finish

    def rows_of_p(i):
        return pw[pl.ds(pl.multiple_of(i * 256, 256), 256), :]

    l_finish = feat_scatter(
        lambda i: dot_nt(hr[...], rows_of_p(i)), lcs, lcr, lys, lyr, lc_s, lc_r, ly_s, ly_r
    )
    for d in NEAR_Z:
        mzc[d].wait_recv()
    am = [jnp.concatenate([mz[k, i] for k in range(NZ)], axis=0) for i in range(3)]
    am = [m - jnp.sum(m, axis=0, keepdims=True) * (1.0 / NZ) for m in am]
    bm = (am[2] * 512.0).T.astype(BF16)
    zrows = pl.ds(pl.multiple_of(z * 32, 32), 32)
    for h in range(2):
        mcorr[h] = dot_nn(bm, am[h].astype(BF16))
    total = tp[:, zrows, :].astype(F32) + mcorr[:, zrows, :]
    for d in NEAR_Z:
        tz[d].wait_recv()
        total = total + tzr[d - 1].astype(F32)
    tfull[pl.ds(2 * x, 2), zrows, :] = total.astype(BF16)
    mine = tfull.at[pl.ds(2 * x, 2), zrows, :]
    az = {d: send(mine, mine, az_s.at[d - 1], az_r.at[d - 1], zdev[d]) for d in NEAR_Z}
    ax = {}
    for e in NEAR_4:
        ax[0, e] = send(mine, mine, ax_s.at[0, e - 1], ax_r.at[0, e - 1], xdev[e])

    def forward(zset):
        for d in zset:
            az[d].wait_recv()
            there = tfull.at[pl.ds(2 * x, 2), pl.ds(pl.multiple_of(zback[d] * 32, 32), 32), :]
            for e in NEAR_4:
                ax[d, e] = send(there, there, ax_s.at[d, e - 1], ax_r.at[d, e - 1], xdev[e])

    forward((1, 7))
    total = l_finish()
    la[feat] = total[0:128].astype(BF16)
    lb[...] = total[128:256].astype(BF16)
    la_forward, la_finish = feat_gather(lambda i: la.at[i], lay_s, lay_r, lac_s, lac_r)
    forward((2, 6))
    la_forward()
    forward((3, 5, 4))
    la_finish()
    for d in (0,) + NEAR_Z:
        for e in NEAR_4:
            ax[d, e].wait_recv()

    def gram_b():
        zb = sum(dot_nt(la[i], tfull[i]) for i in range(8))
        zall[feat, 128:256, :] = zb.astype(BF16)

    za_finish = feat_scatter(
        lambda i: dot_nn(lb[...], tfull[i]), zcs, zcr, zys, zyr, zc_s, zc_r, zy_s, zy_r, gram_b
    )
    zb_forward, zb_finish = feat_gather(
        lambda i: zall.at[i, pl.ds(128, 128), :], zby_s, zby_r, zbc_s, zbc_r
    )
    zall[feat, 0:128, :] = za_finish().astype(BF16)
    za_forward, za_finish2 = feat_gather(
        lambda i: zall.at[i, pl.ds(0, 128), :], zay_s, zay_r, zac_s, zac_r
    )
    zb_forward()
    za_forward()
    zb_finish()
    za_finish2()

    back[0] = rstd_a
    back[1] = rstd_b
    back[2] = factor

    def gradient(n, carry):
        cols = pl.ds(pl.multiple_of(n * 256, 256), 256)
        g = sum(dot_nn(zall[i], pw[i * 256:(i + 1) * 256, cols]) for i in range(8))
        ra, rb, fac = back[0, :, cols], back[1, :, cols], back[2, :, cols]
        ha, hb = hat[0:128, cols], hat[128:256, cols]
        qa = g[0:128] * ra
        na = coef * qa + hb * fac
        nb = coef * (g[128:256] * rb) + ha * fac
        grad[0:128, cols] = na
        grad[128:256, cols] = nb
        gsx[x, 0, :, cols] = jnp.sum(na, axis=0, keepdims=True)
        gsx[x, 1, :, cols] = jnp.sum(nb, axis=0, keepdims=True)
        gsx[x, 2, :, cols] = jnp.sum(na * ha, axis=0, keepdims=True)
        gsx[x, 3, :, cols] = jnp.sum(nb * hb, axis=0, keepdims=True)
        gsx[x, 4, :, cols] = jnp.sum(qa * ha, axis=0, keepdims=True)
        return carry

    lax.fori_loop(0, 4, gradient, 0)
    gx = {d: send(gsx.at[x], gsx.at[x], gx_s.at[d - 1], gx_r.at[d - 1], xdev[d]) for d in NEAR_4}
    for d in NEAR_4:
        gx[d].wait_recv()
    for i in range(5):
        gsz[z, i] = (gsx[0, i] + gsx[1, i]) + (gsx[2, i] + gsx[3, i])
    gz = {d: send(gsz.at[z], gsz.at[z], gz_s.at[d - 1], gz_r.at[d - 1], zdev[d]) for d in NEAR_Z}
    for d in NEAR_Z:
        gz[d].wait_recv()
    sums = [sum(gsz[k, i] for k in range(NZ)) for i in range(5)]
    means = [s * (1.0 / images) for s in sums[:4]]
    hr[0:128, :] = (rstd_a * (grad[0:128, :] - means[0] - hat[0:128, :] * means[2])).astype(BF16)
    hr[128:256, :] = (rstd_b * (grad[128:256, :] - means[1] - hat[128:256, :] * means[3])).astype(BF16)

    share = diag + (LAMBDA / (images * images)) * jnp.sum(sums[4], axis=1, keepdims=True)
    lo[...] = jnp.broadcast_to(share, (8, 128))
    lc = send(lo, lorc, lo_s.at[0], lo_r.at[0], cdev)
    o_finish = feat_scatter(
        lambda i: dot_nt(hr[...], rows_of_p(i)), ocs, ocr, oys, oyr, oc_s, oc_r, oy_s, oy_r
    )
    lc.wait_recv()
    pair = jnp.where(core == 0, lo[...] + lorc[...], lorc[...] + lo[...])
    lo2[...] = pair
    lly = {d: send(lo2, lory.at[y], lo_s.at[d], lo_r.at[d], ydev[d]) for d in NEAR_4}
    lory[y] = pair
    total = o_finish()
    grads_ref[...] = total.astype(BF16)
    for d in NEAR_4:
        lly[d].wait_recv()
    loss_ref[...] = (lory[0] + lory[1]) + (lory[2] + lory[3])
    for cp in sent:
        cp.wait_send()


def on_device(view_a, view_b, projection):
    dma = pltpu.SemaphoreType.DMA
    vmem = pltpu.VMEM
    scratch = [
        vmem((256, 2048), BF16), vmem((2048, 1024), BF16), vmem((256, 1024), F32),
        vmem((256, 1024), BF16), vmem((256, 1024), F32), vmem((3, 1, 1024), F32),
        vmem((2, 4, 128, 256), BF16), vmem((4, 128, 256), BF16), vmem((2, 256, 256), BF16),
        vmem((7, 2, 32, 256), BF16), vmem((8, 256, 256), BF16),
        vmem((8, 3, 1, 256), F32), vmem((2, 256, 256), F32),
        vmem((4, 5, 1, 1024), F32), vmem((8, 5, 1, 1024), F32),
        vmem((4, 256, 256), BF16), vmem((4, 256, 256), BF16), vmem((3, 256, 256), BF16),
        vmem((3, 256, 256), BF16), vmem((8, 128, 256), BF16), vmem((128, 256), BF16),
        vmem((4, 128, 256), BF16), vmem((4, 128, 256), BF16), vmem((3, 128, 256), BF16),
        vmem((3, 128, 256), BF16), vmem((8, 256, 256), BF16),
        vmem((4, 5, 1, 1024), F32), vmem((8, 5, 1, 1024), F32),
        vmem((4, 256, 256), BF16), vmem((4, 256, 256), BF16), vmem((3, 256, 256), BF16),
        vmem((3, 256, 256), BF16),
        vmem((8, 128), F32), vmem((8, 128), F32), vmem((8, 128), F32), vmem((4, 8, 128), F32),
        dma((3,)),
    ]
    sizes = [
        (3,), (3,), (3,), (7,), (7,), (7,), (8, 3),
        (3,), (7,), (4,), (3,), (3,), (4,),
        (4,), (3,), (3,), (4,), (3,), (4,),
        (3,), (7,), (4,), (3,), (4,),
    ]
    for s in sizes:
        scratch += [dma(s), dma(s)]
    loss, grads = pl.pallas_call(
        kernel,
        out_shape=(
            jax.ShapeDtypeStruct((8, 128), F32),
            jax.ShapeDtypeStruct((256, 256), BF16),
        ),
        in_specs=[pl.BlockSpec(memory_space=pltpu.HBM)] * 3,
        out_specs=[pl.BlockSpec(memory_space=pltpu.VMEM)] * 2,
        scratch_shapes=scratch,
        compiler_params=pltpu.CompilerParams(
            collective_id=0, has_side_effects=True, vmem_limit_bytes=63 * 1024 * 1024
        ),
        cost_estimate=pl.CostEstimate(flops=5 * 10**9, bytes_accessed=6 * 10**6, transcendentals=0),
        name="twins",
    )(view_a, view_b, projection)
    return loss[0, 0], grads[0:128], grads[128:256]


def solution(mesh):
    in_specs = (P("img", None), P("img", None), P(None, "feat"))
    out_specs = (P(), P("img", "feat"), P("img", "feat"))
    return jax.shard_map(
        on_device, mesh=mesh, in_specs=in_specs, out_specs=out_specs, check_vma=False
    )
```

```python
import functools
import jax
import jax.numpy as jnp
from jax import lax
from jax.experimental import pallas as pl
from jax.experimental.pallas import tpu as pltpu
from jax.sharding import PartitionSpec as P

LAMBDA = 0.0051
EPSILON = 1e-05
MESH = pl.DeviceIdType.MESH
NZ, NX, NY = 8, 4, 4
F32, BF16 = jnp.float32, jnp.bfloat16
NEAR_Z = (1, 7, 2, 6, 3, 5, 4)
NEAR_4 = (1, 3, 2)


def remote(src, dst, send_sem, recv_sem, device):
    return pltpu.make_async_remote_copy(
        src_ref=src, dst_ref=dst, send_sem=send_sem, recv_sem=recv_sem,
        device_id=device, device_id_type=MESH,
    )


def dot_nt(a, b):
    return lax.dot_general(a, b, (((1,), (1,)), ((), ())), preferred_element_type=F32)


def dot_nn(a, b):
    return jnp.dot(a, b, preferred_element_type=F32)


def merge(parts, count):
    n = len(parts)
    ma = sum(p[0] for p in parts) * (1.0 / n)
    mb = sum(p[1] for p in parts) * (1.0 / n)
    da = [p[0] - ma for p in parts]
    db = [p[1] - mb for p in parts]
    saa = sum(p[2] for p in parts) + count * sum(d * d for d in da)
    sbb = sum(p[3] for p in parts) + count * sum(d * d for d in db)
    sab = sum(p[4] for p in parts) + count * sum(d * e for d, e in zip(da, db))
    return [ma, mb, saa, sbb, sab]


def kernel(
    va, vb, proj, loss_ref, grads_ref,
    vv, pw, hat, hr, grad, back,
    xa, xb, tp, tzr, tfull, mz, mcorr,
    stx, stz, lcs, lcr, lys, lyr, la, lb,
    zcs, zcr, zys, zyr, zown, zall, gax, gaz, gbx, gbz,
    ocs, ocr, oys, oyr, pcs, pcr, pys, pyr, lo, lorc, lo2, lory,
    in_sem, xa_s, xa_r, xb_s, xb_r, xc_s, xc_r, tz_s, tz_r, mz_s, mz_r, az_s, az_r, ax_s, ax_r,
    sx_s, sx_r, sz_s, sz_r, lc_s, lc_r, ly_s, ly_r, lay_s, lay_r, lac_s, lac_r,
    zc_s, zc_r, zy_s, zy_r, zay_s, zay_r, zac_s, zac_r, zby_s, zby_r, zbc_s, zbc_r,
    gax_s, gax_r, gaz_s, gaz_r, gbx_s, gbx_r, gbz_s, gbz_r, oc_s, oc_r, oy_s, oy_r, pc_s, pc_r, py_s, py_r, lo_s, lo_r,
):
    images = 128 * NZ * NX
    img, feat = lax.axis_index("img"), lax.axis_index("feat")
    z, x = lax.div(img, NX), lax.rem(img, NX)
    y, core = lax.div(feat, 2), lax.rem(feat, 2)
    zs = [lax.rem(z + d, NZ) for d in range(NZ)]
    xs = [lax.rem(x + d, NX) for d in range(NX)]
    ys = [lax.rem(y + d, NY) for d in range(NY)]
    xback = [lax.rem(x + NX - d, NX) for d in range(NX)]
    yback = [lax.rem(y + NY - d, NY) for d in range(NY)]
    zback = [lax.rem(z + NZ - d, NZ) for d in range(NZ)]
    zdev = [(v * NX + x, feat) for v in zs]
    xdev = [(z * NX + v, feat) for v in xs]
    ydev = [(img, v * 2 + core) for v in ys]
    cdev = (img, y * 2 + 1 - core)

    loads = [
        pltpu.make_async_copy(va, vv.at[pl.ds(0, 128)], in_sem.at[0]),
        pltpu.make_async_copy(vb, vv.at[pl.ds(128, 128)], in_sem.at[1]),
        pltpu.make_async_copy(proj, pw, in_sem.at[2]),
    ]
    for cp in loads:
        cp.start()
    barrier = pltpu.get_barrier_semaphore()
    peers = zdev[1:] + xdev[1:] + ydev[1:] + [cdev]
    for peer in peers:
        pl.semaphore_signal(barrier, inc=1, device_id=peer, device_id_type=MESH)

    sent = []

    def send(src, dst, send_sem, recv_sem, device):
        cp = remote(src, dst, send_sem, recv_sem, device)
        cp.start()
        sent.append(cp)
        return cp

    def cols256(i):
        return pl.ds(pl.multiple_of(i * 256, 256), 256)

    pl.semaphore_wait(barrier, len(peers))
    xac, xbc, xcc = {}, {}, {}
    for d in (2, 1, 3):
        xac[d] = send(
            va.at[:, cols256(xs[d] * 2 + core)], xa.at[core, x],
            xa_s.at[d - 1], xa_r.at[d - 1], xdev[d],
        )
        xbc[d] = send(
            vb.at[:, cols256(feat)], xb.at[x],
            xb_s.at[d - 1], xb_r.at[d - 1], xdev[d],
        )

    loads[0].wait()
    loads[1].wait()
    xa[0, x] = vv[0:128, cols256(x * 2)]
    xa[1, x] = vv[0:128, cols256(x * 2 + 1)]
    xb[x] = vv[128:256, cols256(feat)]

    loads[2].wait()

    def project(n, carry):
        cols = pl.ds(pl.multiple_of(n * 256, 256), 256)
        pr = dot_nn(vv[...], pw[:, cols])
        hat[:, cols] = pr
        pa, pb = pr[0:128], pr[128:256]
        ma = jnp.sum(pa, axis=0, keepdims=True) * (1.0 / 128)
        mb = jnp.sum(pb, axis=0, keepdims=True) * (1.0 / 128)
        pa, pb = pa - ma, pb - mb
        stx[x, 0, :, cols] = ma
        stx[x, 1, :, cols] = mb
        stx[x, 2, :, cols] = jnp.sum(pa * pa, axis=0, keepdims=True)
        stx[x, 3, :, cols] = jnp.sum(pb * pb, axis=0, keepdims=True)
        stx[x, 4, :, cols] = jnp.sum(pa * pb, axis=0, keepdims=True)
        return carry

    lax.fori_loop(0, 4, project, 0)
    sx = {d: send(stx.at[x], stx.at[x], sx_s.at[d - 1], sx_r.at[d - 1], xdev[d]) for d in NEAR_4}

    for d in NEAR_4:
        xac[d].wait_recv()
        there = xa.at[core, xback[d]]
        xcc[d] = send(there, there, xc_s.at[d - 1], xc_r.at[d - 1], cdev)
    for d in NEAR_4:
        sx[d].wait_recv()
    merged = merge([[stx[k, i] for i in range(5)] for k in range(NX)], 128.0)
    for i in range(5):
        stz[z, i] = merged[i]
    sz = {d: send(stz.at[z], stz.at[z], sz_s.at[d - 1], sz_r.at[d - 1], zdev[d]) for d in NEAR_Z}

    for d in NEAR_4:
        xbc[d].wait_recv()
    bcols = xb[...].reshape(512, 256).astype(F32)
    bmean = jnp.sum(bcols, axis=0, keepdims=True) * (1.0 / 512)
    ct = (bcols - bmean).T.astype(BF16)
    mz[z, 2] = bmean
    for d in NEAR_4:
        xcc[d].wait_recv()
    for h in range(2):
        acols = xa[h].reshape(512, 256).astype(F32)
        amean = jnp.sum(acols, axis=0, keepdims=True) * (1.0 / 512)
        mz[z, h] = amean
        tp[h] = dot_nn(ct, (acols - amean).astype(BF16)).astype(BF16)
    mzc, tz = {}, {}
    for d in NEAR_Z:
        tz[d] = send(
            tp.at[:, pl.ds(pl.multiple_of(zs[d] * 32, 32), 32), :], tzr.at[d - 1],
            tz_s.at[d - 1], tz_r.at[d - 1], zdev[d],
        )
        mzc[d] = send(mz.at[z], mz.at[z], mz_s.at[d - 1], mz_r.at[d - 1], zdev[d])

    for d in NEAR_Z:
        sz[d].wait_recv()
    mean_a, mean_b, saa, sbb, sab = merge(
        [[stz[k, i] for i in range(5)] for k in range(NZ)], 128.0 * NX
    )
    rstd_a = lax.rsqrt(saa * (1.0 / images) + EPSILON)
    rstd_b = lax.rsqrt(sbb * (1.0 / images) + EPSILON)
    corr = sab * rstd_a * rstd_b * (1.0 / images)
    factor = -2.0 * (1.0 - corr) - 2.0 * LAMBDA * corr
    coef = 2.0 * LAMBDA / images
    diag = jnp.sum((1.0 - corr) ** 2 - LAMBDA * corr * corr, axis=1, keepdims=True)
    hat_a = (hat[0:128, :] - mean_a) * rstd_a
    hat[0:128, :] = hat_a
    hr[0:128, :] = (hat_a * rstd_a).astype(BF16)
    hat_b = (hat[128:256, :] - mean_b) * rstd_b
    hat[128:256, :] = hat_b
    hr[128:256, :] = (hat_b * rstd_b).astype(BF16)

    def feat_scatter(chunk, cs, cr, y_send, y_recv, cs_s, cs_r, ysem_s, ysem_r):
        cc, yc = {}, {}

        def other(d):
            cs[d] = chunk(ys[d] * 2 + 1 - core).astype(BF16)
            cc[d] = send(cs.at[d], cr.at[d], cs_s.at[d], cs_r.at[d], cdev)

        def own(d):
            mine = chunk(ys[d] * 2 + core)
            cc[d].wait_recv()
            y_send[d - 1] = (mine + cr[d].astype(F32)).astype(BF16)
            yc[d] = send(y_send.at[d - 1], y_recv.at[d - 1], ysem_s.at[d - 1], ysem_r.at[d - 1], ydev[d])

        other(2)
        other(1)
        other(3)
        own(2)
        own(1)
        own(3)
        other(0)
        total = chunk(feat)
        cc[0].wait_recv()
        total = total + cr[0].astype(F32)

        def finish():
            out = total
            for d in NEAR_4:
                yc[d].wait_recv()
                out = out + y_recv[d - 1].astype(F32)
            return out

        return finish

    def feat_gather(at, y_s, y_r, c_s, c_r):
        yc = {d: send(at(feat), at(feat), y_s.at[d - 1], y_r.at[d - 1], ydev[d]) for d in NEAR_4}
        cc = {0: send(at(feat), at(feat), c_s.at[0], c_r.at[0], cdev)}

        def forward():
            for d in NEAR_4:
                yc[d].wait_recv()
                there = at(yback[d] * 2 + core)
                cc[d] = send(there, there, c_s.at[d], c_r.at[d], cdev)

        def finish():
            for d in range(4):
                cc[d].wait_recv()

        return forward, finish

    def rows_of_p(i):
        return pw[pl.ds(pl.multiple_of(i * 256, 256), 256), :]

    l_finish = feat_scatter(
        lambda i: dot_nt(hr[...], rows_of_p(i)), lcs, lcr, lys, lyr, lc_s, lc_r, ly_s, ly_r
    )
    for d in NEAR_Z:
        mzc[d].wait_recv()
    am = [jnp.concatenate([mz[k, i] for k in range(NZ)], axis=0) for i in range(3)]
    am = [m - jnp.sum(m, axis=0, keepdims=True) * (1.0 / NZ) for m in am]
    bm = (am[2] * 512.0).T.astype(BF16)
    zrows = pl.ds(pl.multiple_of(z * 32, 32), 32)
    for h in range(2):
        mcorr[h] = dot_nn(bm, am[h].astype(BF16))
    total = tp[:, zrows, :].astype(F32) + mcorr[:, zrows, :]
    for d in NEAR_Z:
        tz[d].wait_recv()
        total = total + tzr[d - 1].astype(F32)
    tfull[pl.ds(2 * x, 2), zrows, :] = total.astype(BF16)
    mine = tfull.at[pl.ds(2 * x, 2), zrows, :]
    az = {d: send(mine, mine, az_s.at[d - 1], az_r.at[d - 1], zdev[d]) for d in NEAR_Z}
    ax = {}
    for e in NEAR_4:
        ax[0, e] = send(mine, mine, ax_s.at[0, e - 1], ax_r.at[0, e - 1], xdev[e])

    def piece(d, e):
        there = tfull.at[pl.ds(2 * x, 2), pl.ds(pl.multiple_of(zback[d] * 32, 32), 32), :]
        ax[d, e] = send(there, there, ax_s.at[d, e - 1], ax_r.at[d, e - 1], xdev[e])

    def forward(zset):
        for d in zset:
            az[d].wait_recv()
            for e in NEAR_4:
                piece(d, e)

    forward((1, 7))
    total = l_finish()
    la[feat] = total[0:128].astype(BF16)
    lb[...] = total[128:256].astype(BF16)
    la_forward, la_finish = feat_gather(lambda i: la.at[i], lay_s, lay_r, lac_s, lac_r)
    forward((2, 6, 3, 5, 4))

    zcc = {}

    def za_other(e):
        zcs[e] = dot_nn(lb[...], tfull[xback[e] * 2 + 1 - core]).astype(BF16)
        zcc[e] = send(zcs.at[e], zcr.at[e], zc_s.at[e], zc_r.at[e], cdev)

    def za_copy(slot, there):
        return remote(
            zys.at[slot], zyr.at[slot], zy_s.at[slot], zy_r.at[slot], (img, there * 2 + core)
        )

    def za_own(e):
        there = xback[e]
        total = dot_nn(lb[...], tfull[there * 2 + core])
        zcc[e].wait_recv()
        total = total + zcr[e].astype(F32)
        slot = jnp.maximum(lax.rem(there - y + NY, NY) - 1, 0)

        @pl.when(there == y)
        def _():
            zown[...] = total

        @pl.when(there != y)
        def _():
            zys[slot] = total.astype(BF16)
            za_copy(slot, there).start()

    def zb_part(e):
        i = xback[e] * 2
        return dot_nt(la[i], tfull[i]) + dot_nt(la[i + 1], tfull[i + 1])

    def quarter(e):
        for d in (0,) + NEAR_Z:
            ax[d, e].wait_recv()

    za_other(0)
    la_forward()
    za_own(0)
    quarter(1)
    za_other(1)
    la_finish()
    zb = zb_part(0)
    za_own(1)
    quarter(3)
    za_other(3)
    zb = zb + zb_part(1)
    za_own(3)
    zb = zb + zb_part(3)
    quarter(2)
    za_other(2)
    zb = zb + zb_part(2)
    za_own(2)
    zall[feat, 128:256, :] = zb.astype(BF16)
    zb_forward, zb_finish = feat_gather(
        lambda i: zall.at[i, pl.ds(128, 128), :], zby_s, zby_r, zbc_s, zbc_r
    )
    for d in NEAR_4:
        za_copy(d - 1, ys[d]).wait_recv()
    total = zown[...] + zyr[0].astype(F32) + zyr[1].astype(F32) + zyr[2].astype(F32)
    zall[feat, 0:128, :] = total.astype(BF16)
    za_forward, za_finish = feat_gather(
        lambda i: zall.at[i, pl.ds(0, 128), :], zay_s, zay_r, zac_s, zac_r
    )
    zb_forward()
    zb_finish()

    back[0] = rstd_a
    back[1] = rstd_b
    back[2] = factor

    def gradient_b(n, carry):
        cols = cols256(n)
        g = sum(dot_nn(zall[i, 128:256, :], pw[i * 256:(i + 1) * 256, cols]) for i in range(8))
        hb = hat[128:256, cols]
        nb = coef * (g * back[1, :, cols]) + hat[0:128, cols] * back[2, :, cols]
        grad[128:256, cols] = nb
        gbx[x, 0, :, cols] = jnp.sum(nb, axis=0, keepdims=True)
        gbx[x, 1, :, cols] = jnp.sum(nb * hb, axis=0, keepdims=True)
        return carry

    def gradient_a(n, carry):
        cols = cols256(n)
        g = sum(dot_nn(zall[i, 0:128, :], pw[i * 256:(i + 1) * 256, cols]) for i in range(8))
        ha = hat[0:128, cols]
        qa = g * back[0, :, cols]
        na = coef * qa + hat[128:256, cols] * back[2, :, cols]
        grad[0:128, cols] = na
        gax[x, 0, :, cols] = jnp.sum(na, axis=0, keepdims=True)
        gax[x, 1, :, cols] = jnp.sum(na * ha, axis=0, keepdims=True)
        gax[x, 2, :, cols] = jnp.sum(qa * ha, axis=0, keepdims=True)
        return carry

    def over_x(buf, s_sem, r_sem):
        return {d: send(buf.at[x], buf.at[x], s_sem.at[d - 1], r_sem.at[d - 1], xdev[d]) for d in NEAR_4}

    def over_z(copies, xbuf, buf, s_sem, r_sem, rows):
        for d in NEAR_4:
            copies[d].wait_recv()
        for i in range(rows):
            buf[z, i] = (xbuf[0, i] + xbuf[1, i]) + (xbuf[2, i] + xbuf[3, i])
        return {d: send(buf.at[z], buf.at[z], s_sem.at[d - 1], r_sem.at[d - 1], zdev[d]) for d in NEAR_Z}

    lax.fori_loop(0, 4, gradient_b, 0)
    bx = over_x(gbx, gbx_s, gbx_r)
    za_forward()
    bz = over_z(bx, gbx, gbz, gbz_s, gbz_r, 2)
    za_finish()
    lax.fori_loop(0, 4, gradient_a, 0)
    ax = over_x(gax, gax_s, gax_r)
    az = over_z(ax, gax, gaz, gaz_s, gaz_r, 3)

    def standard(copies, buf, rows, rstd):
        for d in NEAR_Z:
            copies[d].wait_recv()
        first = sum(buf[k, 0] for k in range(NZ)) * (1.0 / images)
        second = sum(buf[k, 1] for k in range(NZ)) * (1.0 / images)
        hr[rows, :] = (rstd * (grad[rows, :] - first - hat[rows, :] * second)).astype(BF16)

    arows, brows = pl.ds(0, 128), pl.ds(128, 128)
    standard(bz, gbz, brows, rstd_b)
    ob_finish = feat_scatter(
        lambda i: dot_nt(hr[brows, :], rows_of_p(i)), pcs, pcr, pys, pyr, pc_s, pc_r, py_s, py_r
    )
    standard(az, gaz, arows, rstd_a)
    frob = jnp.sum(sum(gaz[k, 2] for k in range(NZ)), axis=1, keepdims=True)
    lo[...] = jnp.broadcast_to(diag + (LAMBDA / (images * images)) * frob, (8, 128))
    lc = send(lo, lorc, lo_s.at[0], lo_r.at[0], cdev)
    oa_finish = feat_scatter(
        lambda i: dot_nt(hr[arows, :], rows_of_p(i)), ocs, ocr, oys, oyr, oc_s, oc_r, oy_s, oy_r
    )
    lc.wait_recv()
    pair = lo[...] + lorc[...]
    lo2[...] = pair
    lly = {d: send(lo2, lory.at[y], lo_s.at[d], lo_r.at[d], ydev[d]) for d in NEAR_4}
    lory[y] = pair
    grads_ref[128:256, :] = ob_finish().astype(BF16)
    grads_ref[0:128, :] = oa_finish().astype(BF16)
    for d in NEAR_4:
        lly[d].wait_recv()
    loss_ref[...] = (lory[0] + lory[1]) + (lory[2] + lory[3])
    for d in NEAR_4:
        za_copy(d - 1, ys[d]).wait_send()
    for cp in sent:
        cp.wait_send()


def on_device(view_a, view_b, projection):
    dma = pltpu.SemaphoreType.DMA
    vmem = pltpu.VMEM
    scratch = [
        vmem((256, 2048), BF16), vmem((2048, 1024), BF16), vmem((256, 1024), F32),
        vmem((256, 1024), BF16), vmem((256, 1024), F32), vmem((3, 1, 1024), F32),
        vmem((2, 4, 128, 256), BF16), vmem((4, 128, 256), BF16), vmem((2, 256, 256), BF16),
        vmem((7, 2, 32, 256), BF16), vmem((8, 256, 256), BF16),
        vmem((8, 3, 1, 256), F32), vmem((2, 256, 256), F32),
        vmem((4, 5, 1, 1024), F32), vmem((8, 5, 1, 1024), F32),
        vmem((4, 256, 256), BF16), vmem((4, 256, 256), BF16), vmem((3, 256, 256), BF16),
        vmem((3, 256, 256), BF16), vmem((8, 128, 256), BF16), vmem((128, 256), BF16),
        vmem((4, 128, 256), BF16), vmem((4, 128, 256), BF16), vmem((3, 128, 256), BF16),
        vmem((3, 128, 256), BF16), vmem((128, 256), F32), vmem((8, 256, 256), BF16),
        vmem((4, 3, 1, 1024), F32), vmem((8, 3, 1, 1024), F32),
        vmem((4, 2, 1, 1024), F32), vmem((8, 2, 1, 1024), F32),
        vmem((4, 128, 256), BF16), vmem((4, 128, 256), BF16), vmem((3, 128, 256), BF16),
        vmem((3, 128, 256), BF16),
        vmem((4, 128, 256), BF16), vmem((4, 128, 256), BF16), vmem((3, 128, 256), BF16),
        vmem((3, 128, 256), BF16),
        vmem((8, 128), F32), vmem((8, 128), F32), vmem((8, 128), F32), vmem((4, 8, 128), F32),
        dma((3,)),
    ]
    sizes = [
        (3,), (3,), (3,), (7,), (7,), (7,), (8, 3),
        (3,), (7,), (4,), (3,), (3,), (4,),
        (4,), (3,), (3,), (4,), (3,), (4,),
        (3,), (7,), (3,), (7,), (4,), (3,), (4,), (3,), (4,),
    ]
    for s in sizes:
        scratch += [dma(s), dma(s)]
    loss, grads = pl.pallas_call(
        kernel,
        out_shape=(
            jax.ShapeDtypeStruct((8, 128), F32),
            jax.ShapeDtypeStruct((256, 256), BF16),
        ),
        in_specs=[pl.BlockSpec(memory_space=pltpu.HBM)] * 3,
        out_specs=[pl.BlockSpec(memory_space=pltpu.VMEM)] * 2,
        scratch_shapes=scratch,
        compiler_params=pltpu.CompilerParams(
            collective_id=0, has_side_effects=True, vmem_limit_bytes=54784 * 1024
        ),
        cost_estimate=pl.CostEstimate(flops=5 * 10**9, bytes_accessed=6 * 10**6, transcendentals=0),
        name="twins",
    )(view_a, view_b, projection)
    return loss[0, 0], grads[0:128], grads[128:256]


def solution(mesh):
    in_specs = (P("img", None), P("img", None), P(None, "feat"))
    out_specs = (P(), P("img", "feat"), P("img", "feat"))
    return jax.shard_map(
        on_device, mesh=mesh, in_specs=in_specs, out_specs=out_specs, check_vma=False
    )
```

```python
import functools
import jax
import jax.numpy as jnp
from jax import lax
from jax.experimental import pallas as pl
from jax.experimental.pallas import tpu as pltpu
from jax.sharding import PartitionSpec as P

LAMBDA = 0.0051
EPSILON = 1e-05
MESH = pl.DeviceIdType.MESH
NZ, NX, NY = 8, 4, 4
F32, BF16 = jnp.float32, jnp.bfloat16
NEAR_Z = (1, 7, 2, 6, 3, 5, 4)
NEAR_4 = (1, 3, 2)


def remote(src, dst, send_sem, recv_sem, device):
    return pltpu.make_async_remote_copy(
        src_ref=src, dst_ref=dst, send_sem=send_sem, recv_sem=recv_sem,
        device_id=device, device_id_type=MESH,
    )


def dot_nt(a, b):
    return lax.dot_general(a, b, (((1,), (1,)), ((), ())), preferred_element_type=F32)


def dot_nn(a, b):
    return jnp.dot(a, b, preferred_element_type=F32)


def merge(parts, count):
    n = len(parts)
    ma = sum(p[0] for p in parts) * (1.0 / n)
    mb = sum(p[1] for p in parts) * (1.0 / n)
    da = [p[0] - ma for p in parts]
    db = [p[1] - mb for p in parts]
    saa = sum(p[2] for p in parts) + count * sum(d * d for d in da)
    sbb = sum(p[3] for p in parts) + count * sum(d * d for d in db)
    sab = sum(p[4] for p in parts) + count * sum(d * e for d, e in zip(da, db))
    return [ma, mb, saa, sbb, sab]


def kernel(
    va, vb, proj, loss_ref, grads_ref,
    vv, pw, hat, hr, grad, back,
    xa, xb, tp, tzr, tfull, mz, mcorr,
    stx, stz, lcs, lcr, lys, lyr, la, lb,
    zcs, zcr, zys, zyr, zown, zall, gax, gaz, gbx, gbz,
    ocs, ocr, oys, oyr, pcs, pcr, pys, pyr, lo, lorc, lo2, lory,
    in_sem, xa_s, xa_r, xb_s, xb_r, xc_s, xc_r, tz_s, tz_r, mz_s, mz_r, az_s, az_r, ax_s, ax_r,
    sx_s, sx_r, sz_s, sz_r, lc_s, lc_r, ly_s, ly_r, lay_s, lay_r, lac_s, lac_r,
    zc_s, zc_r, zy_s, zy_r, zay_s, zay_r, zac_s, zac_r, zby_s, zby_r, zbc_s, zbc_r,
    gax_s, gax_r, gaz_s, gaz_r, gbx_s, gbx_r, gbz_s, gbz_r, oc_s, oc_r, oy_s, oy_r, pc_s, pc_r, py_s, py_r, lo_s, lo_r,
):
    images = 128 * NZ * NX
    img, feat = lax.axis_index("img"), lax.axis_index("feat")
    z, x = lax.div(img, NX), lax.rem(img, NX)
    y, core = lax.div(feat, 2), lax.rem(feat, 2)
    zs = [lax.rem(z + d, NZ) for d in range(NZ)]
    xs = [lax.rem(x + d, NX) for d in range(NX)]
    ys = [lax.rem(y + d, NY) for d in range(NY)]
    xback = [lax.rem(x + NX - d, NX) for d in range(NX)]
    yback = [lax.rem(y + NY - d, NY) for d in range(NY)]
    zback = [lax.rem(z + NZ - d, NZ) for d in range(NZ)]
    zdev = [(v * NX + x, feat) for v in zs]
    xdev = [(z * NX + v, feat) for v in xs]
    ydev = [(img, v * 2 + core) for v in ys]
    cdev = (img, y * 2 + 1 - core)

    loads = [
        pltpu.make_async_copy(va, vv.at[pl.ds(0, 128)], in_sem.at[0]),
        pltpu.make_async_copy(vb, vv.at[pl.ds(128, 128)], in_sem.at[1]),
        pltpu.make_async_copy(proj, pw, in_sem.at[2]),
    ]
    for cp in loads:
        cp.start()
    barrier = pltpu.get_barrier_semaphore()
    peers = zdev[1:] + xdev[1:] + ydev[1:] + [cdev]
    for peer in peers:
        pl.semaphore_signal(barrier, inc=1, device_id=peer, device_id_type=MESH)

    sent = []

    def send(src, dst, send_sem, recv_sem, device):
        cp = remote(src, dst, send_sem, recv_sem, device)
        cp.start()
        sent.append(cp)
        return cp

    def cols256(i):
        return pl.ds(pl.multiple_of(i * 256, 256), 256)

    pl.semaphore_wait(barrier, len(peers))
    xac, xbc, xcc = {}, {}, {}
    for d in (2, 1, 3):
        xac[d] = send(
            va.at[:, cols256(xs[d] * 2 + core)], xa.at[core, x],
            xa_s.at[d - 1], xa_r.at[d - 1], xdev[d],
        )
        xbc[d] = send(
            vb.at[:, cols256(feat)], xb.at[x],
            xb_s.at[d - 1], xb_r.at[d - 1], xdev[d],
        )

    loads[0].wait()
    loads[1].wait()
    xa[0, x] = vv[0:128, cols256(x * 2)]
    xa[1, x] = vv[0:128, cols256(x * 2 + 1)]
    xb[x] = vv[128:256, cols256(feat)]

    loads[2].wait()

    def project(n, carry):
        cols = pl.ds(pl.multiple_of(n * 256, 256), 256)
        pr = dot_nn(vv[...], pw[:, cols])
        hat[:, cols] = pr
        pa, pb = pr[0:128], pr[128:256]
        ma = jnp.sum(pa, axis=0, keepdims=True) * (1.0 / 128)
        mb = jnp.sum(pb, axis=0, keepdims=True) * (1.0 / 128)
        pa, pb = pa - ma, pb - mb
        stx[x, 0, :, cols] = ma
        stx[x, 1, :, cols] = mb
        stx[x, 2, :, cols] = jnp.sum(pa * pa, axis=0, keepdims=True)
        stx[x, 3, :, cols] = jnp.sum(pb * pb, axis=0, keepdims=True)
        stx[x, 4, :, cols] = jnp.sum(pa * pb, axis=0, keepdims=True)
        return carry

    lax.fori_loop(0, 4, project, 0)
    sx = {d: send(stx.at[x], stx.at[x], sx_s.at[d - 1], sx_r.at[d - 1], xdev[d]) for d in NEAR_4}

    for d in NEAR_4:
        xac[d].wait_recv()
        there = xa.at[core, xback[d]]
        xcc[d] = send(there, there, xc_s.at[d - 1], xc_r.at[d - 1], cdev)
    for d in NEAR_4:
        sx[d].wait_recv()
    merged = merge([[stx[k, i] for i in range(5)] for k in range(NX)], 128.0)
    for i in range(5):
        stz[z, i] = merged[i]
    sz = {d: send(stz.at[z], stz.at[z], sz_s.at[d - 1], sz_r.at[d - 1], zdev[d]) for d in NEAR_Z}

    for d in NEAR_4:
        xbc[d].wait_recv()
    bcols = xb[...].reshape(512, 256).astype(F32)
    bmean = jnp.sum(bcols, axis=0, keepdims=True) * (1.0 / 512)
    ct = (bcols - bmean).T.astype(BF16)
    mz[z, 2] = bmean
    mzc, tz = {}, {}
    for i, h in enumerate((core, 1 - core)):
        if i == 1:
            for d in NEAR_4:
                xcc[d].wait_recv()
        acols = xa[h].reshape(512, 256).astype(F32)
        amean = jnp.sum(acols, axis=0, keepdims=True) * (1.0 / 512)
        mz[z, h] = amean
        tp[h] = dot_nn(ct, (acols - amean).astype(BF16)).astype(BF16)
        for d in NEAR_Z:
            tz[d, i] = send(
                tp.at[h, pl.ds(pl.multiple_of(zs[d] * 32, 32), 32), :], tzr.at[d - 1, h],
                tz_s.at[d - 1, i], tz_r.at[d - 1, i], zdev[d],
            )
    for d in NEAR_Z:
        mzc[d] = send(mz.at[z], mz.at[z], mz_s.at[d - 1], mz_r.at[d - 1], zdev[d])

    for d in NEAR_Z:
        sz[d].wait_recv()
    mean_a, mean_b, saa, sbb, sab = merge(
        [[stz[k, i] for i in range(5)] for k in range(NZ)], 128.0 * NX
    )
    rstd_a = lax.rsqrt(saa * (1.0 / images) + EPSILON)
    rstd_b = lax.rsqrt(sbb * (1.0 / images) + EPSILON)
    corr = sab * rstd_a * rstd_b * (1.0 / images)
    factor = -2.0 * (1.0 - corr) - 2.0 * LAMBDA * corr
    coef = 2.0 * LAMBDA / images
    diag = jnp.sum((1.0 - corr) ** 2 - LAMBDA * corr * corr, axis=1, keepdims=True)
    hat_a = (hat[0:128, :] - mean_a) * rstd_a
    hat[0:128, :] = hat_a
    hr[0:128, :] = (hat_a * rstd_a).astype(BF16)
    hat_b = (hat[128:256, :] - mean_b) * rstd_b
    hat[128:256, :] = hat_b
    hr[128:256, :] = (hat_b * rstd_b).astype(BF16)

    for d in NEAR_Z:
        mzc[d].wait_recv()
    am = [jnp.concatenate([mz[k, i] for k in range(NZ)], axis=0) for i in range(3)]
    am = [m - jnp.sum(m, axis=0, keepdims=True) * (1.0 / NZ) for m in am]
    bm = (am[2] * 512.0).T.astype(BF16)
    zrows = pl.ds(pl.multiple_of(z * 32, 32), 32)
    for h in range(2):
        mcorr[h] = dot_nn(bm, am[h].astype(BF16))
    total = tp[:, zrows, :].astype(F32) + mcorr[:, zrows, :]
    for d in NEAR_Z:
        tz[d, 0].wait_recv()
        tz[d, 1].wait_recv()
        total = total + tzr[d - 1].astype(F32)
    tfull[pl.ds(2 * x, 2), zrows, :] = total.astype(BF16)
    mine = tfull.at[pl.ds(2 * x, 2), zrows, :]
    az = {d: send(mine, mine, az_s.at[d - 1], az_r.at[d - 1], zdev[d]) for d in NEAR_Z}
    ax = {}
    for e in NEAR_4:
        ax[0, e] = send(mine, mine, ax_s.at[0, e - 1], ax_r.at[0, e - 1], xdev[e])

    def feat_scatter(chunk, cs, cr, y_send, y_recv, cs_s, cs_r, ysem_s, ysem_r):
        cc, yc = {}, {}

        def other(d):
            cs[d] = chunk(ys[d] * 2 + 1 - core).astype(BF16)
            cc[d] = send(cs.at[d], cr.at[d], cs_s.at[d], cs_r.at[d], cdev)

        def own(d):
            mine = chunk(ys[d] * 2 + core)
            cc[d].wait_recv()
            y_send[d - 1] = (mine + cr[d].astype(F32)).astype(BF16)
            yc[d] = send(y_send.at[d - 1], y_recv.at[d - 1], ysem_s.at[d - 1], ysem_r.at[d - 1], ydev[d])

        other(2)
        other(1)
        other(3)
        own(2)
        own(1)
        own(3)
        other(0)
        total = chunk(feat)
        cc[0].wait_recv()
        total = total + cr[0].astype(F32)

        def finish():
            out = total
            for d in NEAR_4:
                yc[d].wait_recv()
                out = out + y_recv[d - 1].astype(F32)
            return out

        return finish

    def feat_gather(at, y_s, y_r, c_s, c_r):
        yc = {d: send(at(feat), at(feat), y_s.at[d - 1], y_r.at[d - 1], ydev[d]) for d in NEAR_4}
        cc = {0: send(at(feat), at(feat), c_s.at[0], c_r.at[0], cdev)}

        def forward():
            for d in NEAR_4:
                yc[d].wait_recv()
                there = at(yback[d] * 2 + core)
                cc[d] = send(there, there, c_s.at[d], c_r.at[d], cdev)

        def finish():
            for d in range(4):
                cc[d].wait_recv()

        return forward, finish

    def rows_of_p(i):
        return pw[pl.ds(pl.multiple_of(i * 256, 256), 256), :]

    l_finish = feat_scatter(
        lambda i: dot_nt(hr[...], rows_of_p(i)), lcs, lcr, lys, lyr, lc_s, lc_r, ly_s, ly_r
    )
    def piece(d, e):
        there = tfull.at[pl.ds(2 * x, 2), pl.ds(pl.multiple_of(zback[d] * 32, 32), 32), :]
        ax[d, e] = send(there, there, ax_s.at[d, e - 1], ax_r.at[d, e - 1], xdev[e])

    def forward(zset):
        for d in zset:
            az[d].wait_recv()
            for e in NEAR_4:
                piece(d, e)

    forward((1, 7))
    total = l_finish()
    la[feat] = total[0:128].astype(BF16)
    lb[...] = total[128:256].astype(BF16)
    la_forward, la_finish = feat_gather(lambda i: la.at[i], lay_s, lay_r, lac_s, lac_r)
    forward((2, 6, 3, 5, 4))

    zcc = {}

    def za_other(e):
        zcs[e] = dot_nn(lb[...], tfull[xback[e] * 2 + 1 - core]).astype(BF16)
        zcc[e] = send(zcs.at[e], zcr.at[e], zc_s.at[e], zc_r.at[e], cdev)

    def za_copy(slot, there):
        return remote(
            zys.at[slot], zyr.at[slot], zy_s.at[slot], zy_r.at[slot], (img, there * 2 + core)
        )

    def za_own(e):
        there = xback[e]
        total = dot_nn(lb[...], tfull[there * 2 + core])
        zcc[e].wait_recv()
        total = total + zcr[e].astype(F32)
        slot = jnp.maximum(lax.rem(there - y + NY, NY) - 1, 0)

        @pl.when(there == y)
        def _():
            zown[...] = total

        @pl.when(there != y)
        def _():
            zys[slot] = total.astype(BF16)
            za_copy(slot, there).start()

    def zb_part(e):
        i = xback[e] * 2
        return dot_nt(la[i], tfull[i]) + dot_nt(la[i + 1], tfull[i + 1])

    def quarter(e):
        for d in (0,) + NEAR_Z:
            ax[d, e].wait_recv()

    za_other(0)
    la_forward()
    za_own(0)
    quarter(1)
    za_other(1)
    la_finish()
    zb = zb_part(0)
    za_own(1)
    quarter(3)
    za_other(3)
    zb = zb + zb_part(1)
    za_own(3)
    zb = zb + zb_part(3)
    quarter(2)
    za_other(2)
    zb = zb + zb_part(2)
    za_own(2)
    zall[feat, 128:256, :] = zb.astype(BF16)
    zb_forward, zb_finish = feat_gather(
        lambda i: zall.at[i, pl.ds(128, 128), :], zby_s, zby_r, zbc_s, zbc_r
    )
    for d in NEAR_4:
        za_copy(d - 1, ys[d]).wait_recv()
    total = zown[...] + zyr[0].astype(F32) + zyr[1].astype(F32) + zyr[2].astype(F32)
    zall[feat, 0:128, :] = total.astype(BF16)
    za_forward, za_finish = feat_gather(
        lambda i: zall.at[i, pl.ds(0, 128), :], zay_s, zay_r, zac_s, zac_r
    )
    zb_forward()
    zb_finish()

    back[0] = rstd_a
    back[1] = rstd_b
    back[2] = factor

    def gradient_b(n, carry):
        cols = cols256(n)
        g = sum(dot_nn(zall[i, 128:256, :], pw[i * 256:(i + 1) * 256, cols]) for i in range(8))
        hb = hat[128:256, cols]
        nb = coef * (g * back[1, :, cols]) + hat[0:128, cols] * back[2, :, cols]
        grad[128:256, cols] = nb
        gbx[x, 0, :, cols] = jnp.sum(nb, axis=0, keepdims=True)
        gbx[x, 1, :, cols] = jnp.sum(nb * hb, axis=0, keepdims=True)
        return carry

    def gradient_a(n, carry):
        cols = cols256(n)
        g = sum(dot_nn(zall[i, 0:128, :], pw[i * 256:(i + 1) * 256, cols]) for i in range(8))
        ha = hat[0:128, cols]
        qa = g * back[0, :, cols]
        na = coef * qa + hat[128:256, cols] * back[2, :, cols]
        grad[0:128, cols] = na
        gax[x, 0, :, cols] = jnp.sum(na, axis=0, keepdims=True)
        gax[x, 1, :, cols] = jnp.sum(na * ha, axis=0, keepdims=True)
        gax[x, 2, :, cols] = jnp.sum(qa * ha, axis=0, keepdims=True)
        return carry

    def over_x(buf, s_sem, r_sem):
        return {d: send(buf.at[x], buf.at[x], s_sem.at[d - 1], r_sem.at[d - 1], xdev[d]) for d in NEAR_4}

    def over_z(copies, xbuf, buf, s_sem, r_sem, rows):
        for d in NEAR_4:
            copies[d].wait_recv()
        for i in range(rows):
            buf[z, i] = (xbuf[0, i] + xbuf[1, i]) + (xbuf[2, i] + xbuf[3, i])
        return {d: send(buf.at[z], buf.at[z], s_sem.at[d - 1], r_sem.at[d - 1], zdev[d]) for d in NEAR_Z}

    lax.fori_loop(0, 4, gradient_b, 0)
    bx = over_x(gbx, gbx_s, gbx_r)
    za_forward()
    bz = over_z(bx, gbx, gbz, gbz_s, gbz_r, 2)
    za_finish()
    lax.fori_loop(0, 4, gradient_a, 0)
    ax = over_x(gax, gax_s, gax_r)
    az = over_z(ax, gax, gaz, gaz_s, gaz_r, 3)

    def standard(copies, buf, rows, rstd):
        for d in NEAR_Z:
            copies[d].wait_recv()
        first = sum(buf[k, 0] for k in range(NZ)) * (1.0 / images)
        second = sum(buf[k, 1] for k in range(NZ)) * (1.0 / images)
        hr[rows, :] = (rstd * (grad[rows, :] - first - hat[rows, :] * second)).astype(BF16)

    arows, brows = pl.ds(0, 128), pl.ds(128, 128)
    standard(bz, gbz, brows, rstd_b)
    ob_finish = feat_scatter(
        lambda i: dot_nt(hr[brows, :], rows_of_p(i)), pcs, pcr, pys, pyr, pc_s, pc_r, py_s, py_r
    )
    standard(az, gaz, arows, rstd_a)
    frob = jnp.sum(sum(gaz[k, 2] for k in range(NZ)), axis=1, keepdims=True)
    lo[...] = jnp.broadcast_to(diag + (LAMBDA / (images * images)) * frob, (8, 128))
    lc = send(lo, lorc, lo_s.at[0], lo_r.at[0], cdev)
    oa_finish = feat_scatter(
        lambda i: dot_nt(hr[arows, :], rows_of_p(i)), ocs, ocr, oys, oyr, oc_s, oc_r, oy_s, oy_r
    )
    lc.wait_recv()
    pair = lo[...] + lorc[...]
    lo2[...] = pair
    lly = {d: send(lo2, lory.at[y], lo_s.at[d], lo_r.at[d], ydev[d]) for d in NEAR_4}
    lory[y] = pair
    grads_ref[128:256, :] = ob_finish().astype(BF16)
    grads_ref[0:128, :] = oa_finish().astype(BF16)
    for d in NEAR_4:
        lly[d].wait_recv()
    loss_ref[...] = (lory[0] + lory[1]) + (lory[2] + lory[3])
    for d in NEAR_4:
        za_copy(d - 1, ys[d]).wait_send()
    for cp in sent:
        cp.wait_send()


def on_device(view_a, view_b, projection):
    dma = pltpu.SemaphoreType.DMA
    vmem = pltpu.VMEM
    scratch = [
        vmem((256, 2048), BF16), vmem((2048, 1024), BF16), vmem((256, 1024), F32),
        vmem((256, 1024), BF16), vmem((256, 1024), F32), vmem((3, 1, 1024), F32),
        vmem((2, 4, 128, 256), BF16), vmem((4, 128, 256), BF16), vmem((2, 256, 256), BF16),
        vmem((7, 2, 32, 256), BF16), vmem((8, 256, 256), BF16),
        vmem((8, 3, 1, 256), F32), vmem((2, 256, 256), F32),
        vmem((4, 5, 1, 1024), F32), vmem((8, 5, 1, 1024), F32),
        vmem((4, 256, 256), BF16), vmem((4, 256, 256), BF16), vmem((3, 256, 256), BF16),
        vmem((3, 256, 256), BF16), vmem((8, 128, 256), BF16), vmem((128, 256), BF16),
        vmem((4, 128, 256), BF16), vmem((4, 128, 256), BF16), vmem((3, 128, 256), BF16),
        vmem((3, 128, 256), BF16), vmem((128, 256), F32), vmem((8, 256, 256), BF16),
        vmem((4, 3, 1, 1024), F32), vmem((8, 3, 1, 1024), F32),
        vmem((4, 2, 1, 1024), F32), vmem((8, 2, 1, 1024), F32),
        vmem((4, 128, 256), BF16), vmem((4, 128, 256), BF16), vmem((3, 128, 256), BF16),
        vmem((3, 128, 256), BF16),
        vmem((4, 128, 256), BF16), vmem((4, 128, 256), BF16), vmem((3, 128, 256), BF16),
        vmem((3, 128, 256), BF16),
        vmem((8, 128), F32), vmem((8, 128), F32), vmem((8, 128), F32), vmem((4, 8, 128), F32),
        dma((3,)),
    ]
    sizes = [
        (3,), (3,), (3,), (7, 2), (7,), (7,), (8, 3),
        (3,), (7,), (4,), (3,), (3,), (4,),
        (4,), (3,), (3,), (4,), (3,), (4,),
        (3,), (7,), (3,), (7,), (4,), (3,), (4,), (3,), (4,),
    ]
    for s in sizes:
        scratch += [dma(s), dma(s)]
    loss, grads = pl.pallas_call(
        kernel,
        out_shape=(
            jax.ShapeDtypeStruct((8, 128), F32),
            jax.ShapeDtypeStruct((256, 256), BF16),
        ),
        in_specs=[pl.BlockSpec(memory_space=pltpu.HBM)] * 3,
        out_specs=[pl.BlockSpec(memory_space=pltpu.VMEM)] * 2,
        scratch_shapes=scratch,
        compiler_params=pltpu.CompilerParams(
            collective_id=0, has_side_effects=True, vmem_limit_bytes=54784 * 1024
        ),
        cost_estimate=pl.CostEstimate(flops=5 * 10**9, bytes_accessed=6 * 10**6, transcendentals=0),
        name="twins",
    )(view_a, view_b, projection)
    return loss[0, 0], grads[0:128], grads[128:256]


def solution(mesh):
    in_specs = (P("img", None), P("img", None), P(None, "feat"))
    out_specs = (P(), P("img", "feat"), P("img", "feat"))
    return jax.shard_map(
        on_device, mesh=mesh, in_specs=in_specs, out_specs=out_specs, check_vma=False
    )
```

```python
import functools
import jax
import jax.numpy as jnp
from jax import lax
from jax.experimental import pallas as pl
from jax.experimental.pallas import tpu as pltpu
from jax.sharding import PartitionSpec as P

LAMBDA = 0.0051
EPSILON = 1e-05
MESH = pl.DeviceIdType.MESH
NZ, NX, NY = 8, 4, 4
F32, BF16 = jnp.float32, jnp.bfloat16
NEAR_Z = (1, 7, 2, 6, 3, 5, 4)
NEAR_4 = (1, 3, 2)


def remote(src, dst, send_sem, recv_sem, device):
    return pltpu.make_async_remote_copy(
        src_ref=src, dst_ref=dst, send_sem=send_sem, recv_sem=recv_sem,
        device_id=device, device_id_type=MESH,
    )


def dot_nt(a, b):
    return lax.dot_general(a, b, (((1,), (1,)), ((), ())), preferred_element_type=F32)


def dot_nn(a, b):
    return jnp.dot(a, b, preferred_element_type=F32)


def merge(parts, count):
    n = len(parts)
    ma = sum(p[0] for p in parts) * (1.0 / n)
    mb = sum(p[1] for p in parts) * (1.0 / n)
    da = [p[0] - ma for p in parts]
    db = [p[1] - mb for p in parts]
    saa = sum(p[2] for p in parts) + count * sum(d * d for d in da)
    sbb = sum(p[3] for p in parts) + count * sum(d * d for d in db)
    sab = sum(p[4] for p in parts) + count * sum(d * e for d, e in zip(da, db))
    return [ma, mb, saa, sbb, sab]


def kernel(
    va, vb, proj, loss_ref, grads_ref,
    vv, pw, hat, hr, grad, back,
    xa, xb, tp, tzr, tfull, mz, mcorr,
    stx, stz, lcs, lcr, lys, lyr, la, lb,
    zcs, zcr, zys, zyr, zown, zall, gax, gaz, gbx, gbz,
    ocs, ocr, oys, oyr, pcs, pcr, pys, pyr, lo, lorc, lo2, lory,
    in_sem, xa_s, xa_r, xb_s, xb_r, xc_s, xc_r, tz_s, tz_r, mz_s, mz_r, az_s, az_r, ax_s, ax_r,
    sx_s, sx_r, sz_s, sz_r, lc_s, lc_r, ly_s, ly_r, lay_s, lay_r, lac_s, lac_r,
    zc_s, zc_r, zy_s, zy_r, zay_s, zay_r, zac_s, zac_r, zby_s, zby_r, zbc_s, zbc_r,
    gax_s, gax_r, gaz_s, gaz_r, gbx_s, gbx_r, gbz_s, gbz_r, oc_s, oc_r, oy_s, oy_r, pc_s, pc_r, py_s, py_r, lo_s, lo_r,
):
    images = 128 * NZ * NX
    img, feat = lax.axis_index("img"), lax.axis_index("feat")
    z, x = lax.div(img, NX), lax.rem(img, NX)
    y, core = lax.div(feat, 2), lax.rem(feat, 2)
    zs = [lax.rem(z + d, NZ) for d in range(NZ)]
    xs = [lax.rem(x + d, NX) for d in range(NX)]
    ys = [lax.rem(y + d, NY) for d in range(NY)]
    xback = [lax.rem(x + NX - d, NX) for d in range(NX)]
    yback = [lax.rem(y + NY - d, NY) for d in range(NY)]
    zback = [lax.rem(z + NZ - d, NZ) for d in range(NZ)]
    zdev = [(v * NX + x, feat) for v in zs]
    xdev = [(z * NX + v, feat) for v in xs]
    ydev = [(img, v * 2 + core) for v in ys]
    cdev = (img, y * 2 + 1 - core)

    loads = [
        pltpu.make_async_copy(va, vv.at[pl.ds(0, 128)], in_sem.at[0]),
        pltpu.make_async_copy(vb, vv.at[pl.ds(128, 128)], in_sem.at[1]),
        pltpu.make_async_copy(proj, pw, in_sem.at[2]),
    ]
    for cp in loads:
        cp.start()
    barrier = pltpu.get_barrier_semaphore()
    peers = zdev[1:] + xdev[1:] + ydev[1:] + [cdev]
    for peer in peers:
        pl.semaphore_signal(barrier, inc=1, device_id=peer, device_id_type=MESH)

    sent = []

    def send(src, dst, send_sem, recv_sem, device):
        cp = remote(src, dst, send_sem, recv_sem, device)
        cp.start()
        sent.append(cp)
        return cp

    def cols256(i):
        return pl.ds(pl.multiple_of(i * 256, 256), 256)

    pl.semaphore_wait(barrier, len(peers))
    xac, xbc, xcc = {}, {}, {}
    for d in (2, 1, 3):
        xac[d] = send(
            va.at[:, cols256(xs[d] * 2 + core)], xa.at[core, x],
            xa_s.at[d - 1], xa_r.at[d - 1], xdev[d],
        )
        xbc[d] = send(
            vb.at[:, cols256(feat)], xb.at[x],
            xb_s.at[d - 1], xb_r.at[d - 1], xdev[d],
        )

    loads[0].wait()
    loads[1].wait()
    xa[0, x] = vv[0:128, cols256(x * 2)]
    xa[1, x] = vv[0:128, cols256(x * 2 + 1)]
    xb[x] = vv[128:256, cols256(feat)]

    loads[2].wait()

    def project(n, carry):
        cols = pl.ds(pl.multiple_of(n * 256, 256), 256)
        pr = dot_nn(vv[...], pw[:, cols])
        hat[:, cols] = pr
        pa, pb = pr[0:128], pr[128:256]
        ma = jnp.sum(pa, axis=0, keepdims=True) * (1.0 / 128)
        mb = jnp.sum(pb, axis=0, keepdims=True) * (1.0 / 128)
        pa, pb = pa - ma, pb - mb
        stx[x, 0, :, cols] = ma
        stx[x, 1, :, cols] = mb
        stx[x, 2, :, cols] = jnp.sum(pa * pa, axis=0, keepdims=True)
        stx[x, 3, :, cols] = jnp.sum(pb * pb, axis=0, keepdims=True)
        stx[x, 4, :, cols] = jnp.sum(pa * pb, axis=0, keepdims=True)
        return carry

    lax.fori_loop(0, 4, project, 0)
    sx = {d: send(stx.at[x], stx.at[x], sx_s.at[d - 1], sx_r.at[d - 1], xdev[d]) for d in NEAR_4}

    for d in NEAR_4:
        xac[d].wait_recv()
        there = xa.at[core, xback[d]]
        xcc[d] = send(there, there, xc_s.at[d - 1], xc_r.at[d - 1], cdev)
    for d in NEAR_4:
        sx[d].wait_recv()
    merged = merge([[stx[k, i] for i in range(5)] for k in range(NX)], 128.0)
    for i in range(5):
        stz[z, i] = merged[i]
    sz = {d: send(stz.at[z], stz.at[z], sz_s.at[d - 1], sz_r.at[d - 1], zdev[d]) for d in NEAR_Z}

    for d in NEAR_4:
        xbc[d].wait_recv()
    bcols = xb[...].reshape(512, 256).astype(F32)
    bmean = jnp.sum(bcols, axis=0, keepdims=True) * (1.0 / 512)
    ct = (bcols - bmean).T.astype(BF16)
    mz[z, 2] = bmean
    mzc, tz = {}, {}
    for i, h in enumerate((core, 1 - core)):
        if i == 1:
            for d in NEAR_4:
                xcc[d].wait_recv()
        acols = xa[h].reshape(512, 256).astype(F32)
        amean = jnp.sum(acols, axis=0, keepdims=True) * (1.0 / 512)
        mz[z, h] = amean
        tp[h] = dot_nn(ct, (acols - amean).astype(BF16)).astype(BF16)
        for d in NEAR_Z:
            tz[d, i] = send(
                tp.at[h, pl.ds(pl.multiple_of(zs[d] * 32, 32), 32), :], tzr.at[d - 1, h],
                tz_s.at[d - 1, i], tz_r.at[d - 1, i], zdev[d],
            )
    for d in NEAR_Z:
        mzc[d] = send(mz.at[z], mz.at[z], mz_s.at[d - 1], mz_r.at[d - 1], zdev[d])

    for d in NEAR_Z:
        sz[d].wait_recv()
    mean_a, mean_b, saa, sbb, sab = merge(
        [[stz[k, i] for i in range(5)] for k in range(NZ)], 128.0 * NX
    )
    rstd_a = lax.rsqrt(saa * (1.0 / images) + EPSILON)
    rstd_b = lax.rsqrt(sbb * (1.0 / images) + EPSILON)
    corr = sab * rstd_a * rstd_b * (1.0 / images)
    factor = -2.0 * (1.0 - corr) - 2.0 * LAMBDA * corr
    coef = 2.0 * LAMBDA / images
    diag = jnp.sum((1.0 - corr) ** 2 - LAMBDA * corr * corr, axis=1, keepdims=True)
    hat_a = (hat[0:128, :] - mean_a) * rstd_a
    hat[0:128, :] = hat_a
    hr[0:128, :] = (hat_a * rstd_a).astype(BF16)
    hat_b = (hat[128:256, :] - mean_b) * rstd_b
    hat[128:256, :] = hat_b
    hr[128:256, :] = (hat_b * rstd_b).astype(BF16)

    def feat_scatter(chunk, cs, cr, y_send, y_recv, cs_s, cs_r, ysem_s, ysem_r):
        cc, yc = {}, {}

        def other(d):
            cs[d] = chunk(ys[d] * 2 + 1 - core).astype(BF16)
            cc[d] = send(cs.at[d], cr.at[d], cs_s.at[d], cs_r.at[d], cdev)

        def own(d):
            mine = chunk(ys[d] * 2 + core)
            cc[d].wait_recv()
            y_send[d - 1] = (mine + cr[d].astype(F32)).astype(BF16)
            yc[d] = send(y_send.at[d - 1], y_recv.at[d - 1], ysem_s.at[d - 1], ysem_r.at[d - 1], ydev[d])

        other(2)
        other(1)
        other(3)
        own(2)
        own(1)
        own(3)
        other(0)
        total = chunk(feat)
        cc[0].wait_recv()
        total = total + cr[0].astype(F32)

        def finish():
            out = total
            for d in NEAR_4:
                yc[d].wait_recv()
                out = out + y_recv[d - 1].astype(F32)
            return out

        return finish

    def feat_gather(at, y_s, y_r, c_s, c_r):
        yc = {d: send(at(feat), at(feat), y_s.at[d - 1], y_r.at[d - 1], ydev[d]) for d in NEAR_4}
        cc = {0: send(at(feat), at(feat), c_s.at[0], c_r.at[0], cdev)}

        def forward():
            for d in NEAR_4:
                yc[d].wait_recv()
                there = at(yback[d] * 2 + core)
                cc[d] = send(there, there, c_s.at[d], c_r.at[d], cdev)

        def finish():
            for d in range(4):
                cc[d].wait_recv()

        return forward, finish

    def rows_of_p(i):
        return pw[pl.ds(pl.multiple_of(i * 256, 256), 256), :]

    l_finish = feat_scatter(
        lambda i: dot_nt(hr[...], rows_of_p(i)), lcs, lcr, lys, lyr, lc_s, lc_r, ly_s, ly_r
    )
    for d in NEAR_Z:
        mzc[d].wait_recv()
    am = [jnp.concatenate([mz[k, i] for k in range(NZ)], axis=0) for i in range(3)]
    am = [m - jnp.sum(m, axis=0, keepdims=True) * (1.0 / NZ) for m in am]
    bm = (am[2] * 512.0).T.astype(BF16)
    zrows = pl.ds(pl.multiple_of(z * 32, 32), 32)
    for h in range(2):
        mcorr[h] = dot_nn(bm, am[h].astype(BF16))
    total = tp[:, zrows, :].astype(F32) + mcorr[:, zrows, :]
    for d in NEAR_Z:
        tz[d, 0].wait_recv()
        tz[d, 1].wait_recv()
        total = total + tzr[d - 1].astype(F32)
    tfull[pl.ds(2 * x, 2), zrows, :] = total.astype(BF16)
    mine = tfull.at[pl.ds(2 * x, 2), zrows, :]
    az = {d: send(mine, mine, az_s.at[d - 1], az_r.at[d - 1], zdev[d]) for d in NEAR_Z}
    ax = {}
    for e in NEAR_4:
        ax[0, e] = send(mine, mine, ax_s.at[0, e - 1], ax_r.at[0, e - 1], xdev[e])

    def piece(d, e):
        there = tfull.at[pl.ds(2 * x, 2), pl.ds(pl.multiple_of(zback[d] * 32, 32), 32), :]
        ax[d, e] = send(there, there, ax_s.at[d, e - 1], ax_r.at[d, e - 1], xdev[e])

    def forward(zset):
        for d in zset:
            az[d].wait_recv()
            for e in NEAR_4:
                piece(d, e)

    forward((1, 7, 2, 6))
    total = l_finish()
    la[feat] = total[0:128].astype(BF16)
    lb[...] = total[128:256].astype(BF16)
    la_forward, la_finish = feat_gather(lambda i: la.at[i], lay_s, lay_r, lac_s, lac_r)
    forward((3, 5, 4))

    zcc = {}

    def za_other(e):
        zcs[e] = dot_nn(lb[...], tfull[xback[e] * 2 + 1 - core]).astype(BF16)
        zcc[e] = send(zcs.at[e], zcr.at[e], zc_s.at[e], zc_r.at[e], cdev)

    def za_copy(slot, there):
        return remote(
            zys.at[slot], zyr.at[slot], zy_s.at[slot], zy_r.at[slot], (img, there * 2 + core)
        )

    def za_own(e):
        there = xback[e]
        total = dot_nn(lb[...], tfull[there * 2 + core])
        zcc[e].wait_recv()
        total = total + zcr[e].astype(F32)
        slot = jnp.maximum(lax.rem(there - y + NY, NY) - 1, 0)

        @pl.when(there == y)
        def _():
            zown[...] = total

        @pl.when(there != y)
        def _():
            zys[slot] = total.astype(BF16)
            za_copy(slot, there).start()

    def zb_part(e):
        i = xback[e] * 2
        return dot_nt(la[i], tfull[i]) + dot_nt(la[i + 1], tfull[i + 1])

    def quarter(e):
        for d in (0,) + NEAR_Z:
            ax[d, e].wait_recv()

    za_other(0)
    la_forward()
    za_own(0)
    quarter(1)
    za_other(1)
    la_finish()
    zb = zb_part(0)
    za_own(1)
    quarter(3)
    za_other(3)
    zb = zb + zb_part(1)
    za_own(3)
    zb = zb + zb_part(3)
    quarter(2)
    za_other(2)
    zb = zb + zb_part(2)
    za_own(2)
    zall[feat, 128:256, :] = zb.astype(BF16)
    zb_forward, zb_finish = feat_gather(
        lambda i: zall.at[i, pl.ds(128, 128), :], zby_s, zby_r, zbc_s, zbc_r
    )
    for d in NEAR_4:
        za_copy(d - 1, ys[d]).wait_recv()
    total = zown[...] + zyr[0].astype(F32) + zyr[1].astype(F32) + zyr[2].astype(F32)
    zall[feat, 0:128, :] = total.astype(BF16)
    za_forward, za_finish = feat_gather(
        lambda i: zall.at[i, pl.ds(0, 128), :], zay_s, zay_r, zac_s, zac_r
    )
    zb_forward()
    zb_finish()

    back[0] = rstd_a
    back[1] = rstd_b
    back[2] = factor

    def gradient_b(n, carry):
        cols = cols256(n)
        g = sum(dot_nn(zall[i, 128:256, :], pw[i * 256:(i + 1) * 256, cols]) for i in range(8))
        hb = hat[128:256, cols]
        nb = coef * (g * back[1, :, cols]) + hat[0:128, cols] * back[2, :, cols]
        grad[128:256, cols] = nb
        gbx[x, 0, :, cols] = jnp.sum(nb, axis=0, keepdims=True)
        gbx[x, 1, :, cols] = jnp.sum(nb * hb, axis=0, keepdims=True)
        return carry

    def gradient_a(n, carry):
        cols = cols256(n)
        g = sum(dot_nn(zall[i, 0:128, :], pw[i * 256:(i + 1) * 256, cols]) for i in range(8))
        ha = hat[0:128, cols]
        qa = g * back[0, :, cols]
        na = coef * qa + hat[128:256, cols] * back[2, :, cols]
        grad[0:128, cols] = na
        gax[x, 0, :, cols] = jnp.sum(na, axis=0, keepdims=True)
        gax[x, 1, :, cols] = jnp.sum(na * ha, axis=0, keepdims=True)
        gax[x, 2, :, cols] = jnp.sum(qa * ha, axis=0, keepdims=True)
        return carry

    def over_x(buf, s_sem, r_sem):
        return {d: send(buf.at[x], buf.at[x], s_sem.at[d - 1], r_sem.at[d - 1], xdev[d]) for d in NEAR_4}

    def over_z(copies, xbuf, buf, s_sem, r_sem, rows):
        for d in NEAR_4:
            copies[d].wait_recv()
        for i in range(rows):
            buf[z, i] = (xbuf[0, i] + xbuf[1, i]) + (xbuf[2, i] + xbuf[3, i])
        return {d: send(buf.at[z], buf.at[z], s_sem.at[d - 1], r_sem.at[d - 1], zdev[d]) for d in NEAR_Z}

    lax.fori_loop(0, 4, gradient_b, 0)
    bx = over_x(gbx, gbx_s, gbx_r)
    za_forward()
    bz = over_z(bx, gbx, gbz, gbz_s, gbz_r, 2)
    za_finish()
    lax.fori_loop(0, 4, gradient_a, 0)
    ax = over_x(gax, gax_s, gax_r)
    az = over_z(ax, gax, gaz, gaz_s, gaz_r, 3)

    def standard(copies, buf, rows, rstd):
        for d in NEAR_Z:
            copies[d].wait_recv()
        first = sum(buf[k, 0] for k in range(NZ)) * (1.0 / images)
        second = sum(buf[k, 1] for k in range(NZ)) * (1.0 / images)
        hr[rows, :] = (rstd * (grad[rows, :] - first - hat[rows, :] * second)).astype(BF16)

    arows, brows = pl.ds(0, 128), pl.ds(128, 128)
    standard(bz, gbz, brows, rstd_b)
    ob_finish = feat_scatter(
        lambda i: dot_nt(hr[brows, :], rows_of_p(i)), pcs, pcr, pys, pyr, pc_s, pc_r, py_s, py_r
    )
    standard(az, gaz, arows, rstd_a)
    frob = jnp.sum(sum(gaz[k, 2] for k in range(NZ)), axis=1, keepdims=True)
    lo[...] = jnp.broadcast_to(diag + (LAMBDA / (images * images)) * frob, (8, 128))
    lc = send(lo, lorc, lo_s.at[0], lo_r.at[0], cdev)
    oa_finish = feat_scatter(
        lambda i: dot_nt(hr[arows, :], rows_of_p(i)), ocs, ocr, oys, oyr, oc_s, oc_r, oy_s, oy_r
    )
    lc.wait_recv()
    pair = lo[...] + lorc[...]
    lo2[...] = pair
    lly = {d: send(lo2, lory.at[y], lo_s.at[d], lo_r.at[d], ydev[d]) for d in NEAR_4}
    lory[y] = pair
    grads_ref[128:256, :] = ob_finish().astype(BF16)
    grads_ref[0:128, :] = oa_finish().astype(BF16)
    for d in NEAR_4:
        lly[d].wait_recv()
    loss_ref[...] = (lory[0] + lory[1]) + (lory[2] + lory[3])
    for d in NEAR_4:
        za_copy(d - 1, ys[d]).wait_send()
    for cp in sent:
        cp.wait_send()


def on_device(view_a, view_b, projection):
    dma = pltpu.SemaphoreType.DMA
    vmem = pltpu.VMEM
    scratch = [
        vmem((256, 2048), BF16), vmem((2048, 1024), BF16), vmem((256, 1024), F32),
        vmem((256, 1024), BF16), vmem((256, 1024), F32), vmem((3, 1, 1024), F32),
        vmem((2, 4, 128, 256), BF16), vmem((4, 128, 256), BF16), vmem((2, 256, 256), BF16),
        vmem((7, 2, 32, 256), BF16), vmem((8, 256, 256), BF16),
        vmem((8, 3, 1, 256), F32), vmem((2, 256, 256), F32),
        vmem((4, 5, 1, 1024), F32), vmem((8, 5, 1, 1024), F32),
        vmem((4, 256, 256), BF16), vmem((4, 256, 256), BF16), vmem((3, 256, 256), BF16),
        vmem((3, 256, 256), BF16), vmem((8, 128, 256), BF16), vmem((128, 256), BF16),
        vmem((4, 128, 256), BF16), vmem((4, 128, 256), BF16), vmem((3, 128, 256), BF16),
        vmem((3, 128, 256), BF16), vmem((128, 256), F32), vmem((8, 256, 256), BF16),
        vmem((4, 3, 1, 1024), F32), vmem((8, 3, 1, 1024), F32),
        vmem((4, 2, 1, 1024), F32), vmem((8, 2, 1, 1024), F32),
        vmem((4, 128, 256), BF16), vmem((4, 128, 256), BF16), vmem((3, 128, 256), BF16),
        vmem((3, 128, 256), BF16),
        vmem((4, 128, 256), BF16), vmem((4, 128, 256), BF16), vmem((3, 128, 256), BF16),
        vmem((3, 128, 256), BF16),
        vmem((8, 128), F32), vmem((8, 128), F32), vmem((8, 128), F32), vmem((4, 8, 128), F32),
        dma((3,)),
    ]
    sizes = [
        (3,), (3,), (3,), (7, 2), (7,), (7,), (8, 3),
        (3,), (7,), (4,), (3,), (3,), (4,),
        (4,), (3,), (3,), (4,), (3,), (4,),
        (3,), (7,), (3,), (7,), (4,), (3,), (4,), (3,), (4,),
    ]
    for s in sizes:
        scratch += [dma(s), dma(s)]
    loss, grads = pl.pallas_call(
        kernel,
        out_shape=(
            jax.ShapeDtypeStruct((8, 128), F32),
            jax.ShapeDtypeStruct((256, 256), BF16),
        ),
        in_specs=[pl.BlockSpec(memory_space=pltpu.HBM)] * 3,
        out_specs=[pl.BlockSpec(memory_space=pltpu.VMEM)] * 2,
        scratch_shapes=scratch,
        compiler_params=pltpu.CompilerParams(
            collective_id=0, has_side_effects=True, vmem_limit_bytes=54784 * 1024
        ),
        cost_estimate=pl.CostEstimate(flops=5 * 10**9, bytes_accessed=6 * 10**6, transcendentals=0),
        name="twins",
    )(view_a, view_b, projection)
    return loss[0, 0], grads[0:128], grads[128:256]


def solution(mesh):
    in_specs = (P("img", None), P("img", None), P(None, "feat"))
    out_specs = (P(), P("img", "feat"), P("img", "feat"))
    return jax.shard_map(
        on_device, mesh=mesh, in_specs=in_specs, out_specs=out_specs, check_vma=False
    )
```

```python
import functools
import jax
import jax.numpy as jnp
from jax import lax
from jax.experimental import pallas as pl
from jax.experimental.pallas import tpu as pltpu
from jax.sharding import PartitionSpec as P

LAMBDA = 0.0051
EPSILON = 1e-05
MESH = pl.DeviceIdType.MESH
NZ, NX, NY = 8, 4, 4
F32, BF16 = jnp.float32, jnp.bfloat16
NEAR_Z = (1, 7, 2, 6, 3, 5, 4)
NEAR_4 = (1, 3, 2)


def remote(src, dst, send_sem, recv_sem, device):
    return pltpu.make_async_remote_copy(
        src_ref=src, dst_ref=dst, send_sem=send_sem, recv_sem=recv_sem,
        device_id=device, device_id_type=MESH,
    )


def dot_nt(a, b):
    return lax.dot_general(a, b, (((1,), (1,)), ((), ())), preferred_element_type=F32)


def dot_nn(a, b):
    return jnp.dot(a, b, preferred_element_type=F32)


def merge(parts, count):
    n = len(parts)
    ma = sum(p[0] for p in parts) * (1.0 / n)
    mb = sum(p[1] for p in parts) * (1.0 / n)
    da = [p[0] - ma for p in parts]
    db = [p[1] - mb for p in parts]
    saa = sum(p[2] for p in parts) + count * sum(d * d for d in da)
    sbb = sum(p[3] for p in parts) + count * sum(d * d for d in db)
    sab = sum(p[4] for p in parts) + count * sum(d * e for d, e in zip(da, db))
    return [ma, mb, saa, sbb, sab]


def kernel(
    va, vb, proj, loss_ref, grads_ref,
    vv, pw, hat, hr, grad, back,
    xa, xb, tp, tzr, tfull, mz, mcorr,
    stx, stz, lcs, lcr, lys, lyr, la, lb,
    zcs, zcr, zys, zyr, zown, zall, gax, gaz, gbx, gbz,
    ocs, ocr, oys, oyr, pcs, pcr, pys, pyr, lo, lorc, lo2, lory,
    in_sem, xa_s, xa_r, xb_s, xb_r, xc_s, xc_r, tz_s, tz_r, mz_s, mz_r, az_s, az_r, ax_s, ax_r,
    sx_s, sx_r, sz_s, sz_r, lc_s, lc_r, ly_s, ly_r, lay_s, lay_r, lac_s, lac_r,
    zc_s, zc_r, zy_s, zy_r, zay_s, zay_r, zac_s, zac_r, zby_s, zby_r, zbc_s, zbc_r,
    gax_s, gax_r, gaz_s, gaz_r, gbx_s, gbx_r, gbz_s, gbz_r, oc_s, oc_r, oy_s, oy_r, pc_s, pc_r, py_s, py_r, lo_s, lo_r,
):
    images = 128 * NZ * NX
    img, feat = lax.axis_index("img"), lax.axis_index("feat")
    z, x = lax.div(img, NX), lax.rem(img, NX)
    y, core = lax.div(feat, 2), lax.rem(feat, 2)
    zs = [lax.rem(z + d, NZ) for d in range(NZ)]
    xs = [lax.rem(x + d, NX) for d in range(NX)]
    ys = [lax.rem(y + d, NY) for d in range(NY)]
    xback = [lax.rem(x + NX - d, NX) for d in range(NX)]
    yback = [lax.rem(y + NY - d, NY) for d in range(NY)]
    zback = [lax.rem(z + NZ - d, NZ) for d in range(NZ)]
    zdev = [(v * NX + x, feat) for v in zs]
    xdev = [(z * NX + v, feat) for v in xs]
    ydev = [(img, v * 2 + core) for v in ys]
    cdev = (img, y * 2 + 1 - core)

    loads = [
        pltpu.make_async_copy(va, vv.at[pl.ds(0, 128)], in_sem.at[0]),
        pltpu.make_async_copy(vb, vv.at[pl.ds(128, 128)], in_sem.at[1]),
        pltpu.make_async_copy(proj, pw, in_sem.at[2]),
    ]
    for cp in loads:
        cp.start()
    barrier = pltpu.get_barrier_semaphore()
    peers = zdev[1:] + xdev[1:] + ydev[1:] + [cdev]
    for peer in peers:
        pl.semaphore_signal(barrier, inc=1, device_id=peer, device_id_type=MESH)

    sent = []

    def send(src, dst, send_sem, recv_sem, device):
        cp = remote(src, dst, send_sem, recv_sem, device)
        cp.start()
        sent.append(cp)
        return cp

    def cols256(i):
        return pl.ds(pl.multiple_of(i * 256, 256), 256)

    pl.semaphore_wait(barrier, len(peers))
    xac, xbc, xcc = {}, {}, {}
    for d in (2, 1, 3):
        xac[d] = send(
            va.at[:, cols256(xs[d] * 2 + core)], xa.at[core, x],
            xa_s.at[d - 1], xa_r.at[d - 1], xdev[d],
        )
        xbc[d] = send(
            vb.at[:, cols256(feat)], xb.at[x],
            xb_s.at[d - 1], xb_r.at[d - 1], xdev[d],
        )

    loads[0].wait()
    loads[1].wait()
    xa[0, x] = vv[0:128, cols256(x * 2)]
    xa[1, x] = vv[0:128, cols256(x * 2 + 1)]
    xb[x] = vv[128:256, cols256(feat)]

    loads[2].wait()

    def project(n, carry):
        cols = pl.ds(pl.multiple_of(n * 256, 256), 256)
        pr = dot_nn(vv[...], pw[:, cols])
        hat[:, cols] = pr
        pa, pb = pr[0:128], pr[128:256]
        ma = jnp.sum(pa, axis=0, keepdims=True) * (1.0 / 128)
        mb = jnp.sum(pb, axis=0, keepdims=True) * (1.0 / 128)
        pa, pb = pa - ma, pb - mb
        stx[x, 0, :, cols] = ma
        stx[x, 1, :, cols] = mb
        stx[x, 2, :, cols] = jnp.sum(pa * pa, axis=0, keepdims=True)
        stx[x, 3, :, cols] = jnp.sum(pb * pb, axis=0, keepdims=True)
        stx[x, 4, :, cols] = jnp.sum(pa * pb, axis=0, keepdims=True)
        return carry

    lax.fori_loop(0, 4, project, 0)
    sx = {d: send(stx.at[x], stx.at[x], sx_s.at[d - 1], sx_r.at[d - 1], xdev[d]) for d in NEAR_4}

    for d in NEAR_4:
        xac[d].wait_recv()
        there = xa.at[core, xback[d]]
        xcc[d] = send(there, there, xc_s.at[d - 1], xc_r.at[d - 1], cdev)
    for d in NEAR_4:
        sx[d].wait_recv()
    merged = merge([[stx[k, i] for i in range(5)] for k in range(NX)], 128.0)
    for i in range(5):
        stz[z, i] = merged[i]
    sz = {d: send(stz.at[z], stz.at[z], sz_s.at[d - 1], sz_r.at[d - 1], zdev[d]) for d in NEAR_Z}

    for d in NEAR_4:
        xbc[d].wait_recv()
    bcols = xb[...].reshape(512, 256).astype(F32)
    bmean = jnp.sum(bcols, axis=0, keepdims=True) * (1.0 / 512)
    ct = (bcols - bmean).T.astype(BF16)
    mz[z, 2] = bmean
    mzc, tz = {}, {}
    for i, h in enumerate((core, 1 - core)):
        if i == 1:
            for d in NEAR_4:
                xcc[d].wait_recv()
        acols = xa[h].reshape(512, 256).astype(F32)
        amean = jnp.sum(acols, axis=0, keepdims=True) * (1.0 / 512)
        mz[z, h] = amean
        tp[h] = dot_nn(ct, (acols - amean).astype(BF16)).astype(BF16)
        for d in NEAR_Z:
            tz[d, i] = send(
                tp.at[h, pl.ds(pl.multiple_of(zs[d] * 32, 32), 32), :], tzr.at[d - 1, h],
                tz_s.at[d - 1, i], tz_r.at[d - 1, i], zdev[d],
            )
    for d in NEAR_Z:
        mzc[d] = send(mz.at[z], mz.at[z], mz_s.at[d - 1], mz_r.at[d - 1], zdev[d])

    for d in NEAR_Z:
        sz[d].wait_recv()
    mean_a, mean_b, saa, sbb, sab = merge(
        [[stz[k, i] for i in range(5)] for k in range(NZ)], 128.0 * NX
    )
    rstd_a = lax.rsqrt(saa * (1.0 / images) + EPSILON)
    rstd_b = lax.rsqrt(sbb * (1.0 / images) + EPSILON)
    corr = sab * rstd_a * rstd_b * (1.0 / images)
    factor = -2.0 * (1.0 - corr) - 2.0 * LAMBDA * corr
    coef = 2.0 * LAMBDA / images
    diag = jnp.sum((1.0 - corr) ** 2 - LAMBDA * corr * corr, axis=1, keepdims=True)
    hat_a = (hat[0:128, :] - mean_a) * rstd_a
    hat[0:128, :] = hat_a
    hr[0:128, :] = (hat_a * rstd_a).astype(BF16)
    hat_b = (hat[128:256, :] - mean_b) * rstd_b
    hat[128:256, :] = hat_b
    hr[128:256, :] = (hat_b * rstd_b).astype(BF16)

    def feat_scatter(chunk, cs, cr, y_send, y_recv, cs_s, cs_r, ysem_s, ysem_r):
        cc, yc = {}, {}

        def other(d):
            cs[d] = chunk(ys[d] * 2 + 1 - core).astype(BF16)
            cc[d] = send(cs.at[d], cr.at[d], cs_s.at[d], cs_r.at[d], cdev)

        def own(d):
            mine = chunk(ys[d] * 2 + core)
            cc[d].wait_recv()
            y_send[d - 1] = (mine + cr[d].astype(F32)).astype(BF16)
            yc[d] = send(y_send.at[d - 1], y_recv.at[d - 1], ysem_s.at[d - 1], ysem_r.at[d - 1], ydev[d])

        other(2)
        other(1)
        other(3)
        other(0)
        own(2)
        own(1)
        own(3)
        total = chunk(feat)
        cc[0].wait_recv()
        total = total + cr[0].astype(F32)

        def finish():
            out = total
            for d in NEAR_4:
                yc[d].wait_recv()
                out = out + y_recv[d - 1].astype(F32)
            return out

        return finish

    def feat_gather(at, y_s, y_r, c_s, c_r):
        yc = {d: send(at(feat), at(feat), y_s.at[d - 1], y_r.at[d - 1], ydev[d]) for d in NEAR_4}
        cc = {0: send(at(feat), at(feat), c_s.at[0], c_r.at[0], cdev)}

        def forward():
            for d in NEAR_4:
                yc[d].wait_recv()
                there = at(yback[d] * 2 + core)
                cc[d] = send(there, there, c_s.at[d], c_r.at[d], cdev)

        def finish():
            for d in range(4):
                cc[d].wait_recv()

        return forward, finish

    def rows_of_p(i):
        return pw[pl.ds(pl.multiple_of(i * 256, 256), 256), :]

    l_finish = feat_scatter(
        lambda i: dot_nt(hr[...], rows_of_p(i)), lcs, lcr, lys, lyr, lc_s, lc_r, ly_s, ly_r
    )
    for d in NEAR_Z:
        mzc[d].wait_recv()
    am = [jnp.concatenate([mz[k, i] for k in range(NZ)], axis=0) for i in range(3)]
    am = [m - jnp.sum(m, axis=0, keepdims=True) * (1.0 / NZ) for m in am]
    bm = (am[2] * 512.0).T.astype(BF16)
    zrows = pl.ds(pl.multiple_of(z * 32, 32), 32)
    for h in range(2):
        mcorr[h] = dot_nn(bm, am[h].astype(BF16))
    total = tp[:, zrows, :].astype(F32) + mcorr[:, zrows, :]
    for d in NEAR_Z:
        tz[d, 0].wait_recv()
        tz[d, 1].wait_recv()
        total = total + tzr[d - 1].astype(F32)
    tfull[pl.ds(2 * x, 2), zrows, :] = total.astype(BF16)
    mine = tfull.at[pl.ds(2 * x, 2), zrows, :]
    az = {d: send(mine, mine, az_s.at[d - 1], az_r.at[d - 1], zdev[d]) for d in NEAR_Z}
    ax = {}
    for e in NEAR_4:
        ax[0, e] = send(mine, mine, ax_s.at[0, e - 1], ax_r.at[0, e - 1], xdev[e])

    def piece(d, e):
        there = tfull.at[pl.ds(2 * x, 2), pl.ds(pl.multiple_of(zback[d] * 32, 32), 32), :]
        ax[d, e] = send(there, there, ax_s.at[d, e - 1], ax_r.at[d, e - 1], xdev[e])

    def forward(zset):
        for d in zset:
            az[d].wait_recv()
            for e in NEAR_4:
                piece(d, e)

    forward((1, 7, 2, 6))
    total = l_finish()
    la[feat] = total[0:128].astype(BF16)
    lb[...] = total[128:256].astype(BF16)
    la_forward, la_finish = feat_gather(lambda i: la.at[i], lay_s, lay_r, lac_s, lac_r)
    forward((3, 5, 4))

    zcc = {}

    def za_other(e):
        zcs[e] = dot_nn(lb[...], tfull[xback[e] * 2 + 1 - core]).astype(BF16)
        zcc[e] = send(zcs.at[e], zcr.at[e], zc_s.at[e], zc_r.at[e], cdev)

    def za_copy(slot, there):
        return remote(
            zys.at[slot], zyr.at[slot], zy_s.at[slot], zy_r.at[slot], (img, there * 2 + core)
        )

    def za_own(e):
        there = xback[e]
        total = dot_nn(lb[...], tfull[there * 2 + core])
        zcc[e].wait_recv()
        total = total + zcr[e].astype(F32)
        slot = jnp.maximum(lax.rem(there - y + NY, NY) - 1, 0)

        @pl.when(there == y)
        def _():
            zown[...] = total

        @pl.when(there != y)
        def _():
            zys[slot] = total.astype(BF16)
            za_copy(slot, there).start()

    def zb_part(e):
        i = xback[e] * 2
        return dot_nt(la[i], tfull[i]) + dot_nt(la[i + 1], tfull[i + 1])

    def quarter(e):
        for d in (0,) + NEAR_Z:
            ax[d, e].wait_recv()

    za_other(0)
    la_forward()
    za_own(0)
    quarter(1)
    za_other(1)
    la_finish()
    zb = zb_part(0)
    za_own(1)
    quarter(3)
    za_other(3)
    zb = zb + zb_part(1)
    za_own(3)
    zb = zb + zb_part(3)
    quarter(2)
    za_other(2)
    zb = zb + zb_part(2)
    za_own(2)
    zall[feat, 128:256, :] = zb.astype(BF16)
    zb_forward, zb_finish = feat_gather(
        lambda i: zall.at[i, pl.ds(128, 128), :], zby_s, zby_r, zbc_s, zbc_r
    )
    for d in NEAR_4:
        za_copy(d - 1, ys[d]).wait_recv()
    total = zown[...] + zyr[0].astype(F32) + zyr[1].astype(F32) + zyr[2].astype(F32)
    zall[feat, 0:128, :] = total.astype(BF16)
    za_forward, za_finish = feat_gather(
        lambda i: zall.at[i, pl.ds(0, 128), :], zay_s, zay_r, zac_s, zac_r
    )
    zb_forward()
    zb_finish()

    back[0] = rstd_a
    back[1] = rstd_b
    back[2] = factor

    def gradient_b(n, carry):
        cols = cols256(n)
        g = sum(dot_nn(zall[i, 128:256, :], pw[i * 256:(i + 1) * 256, cols]) for i in range(8))
        hb = hat[128:256, cols]
        nb = coef * (g * back[1, :, cols]) + hat[0:128, cols] * back[2, :, cols]
        grad[128:256, cols] = nb
        gbx[x, 0, :, cols] = jnp.sum(nb, axis=0, keepdims=True)
        gbx[x, 1, :, cols] = jnp.sum(nb * hb, axis=0, keepdims=True)
        return carry

    def gradient_a(n, carry):
        cols = cols256(n)
        g = sum(dot_nn(zall[i, 0:128, :], pw[i * 256:(i + 1) * 256, cols]) for i in range(8))
        ha = hat[0:128, cols]
        qa = g * back[0, :, cols]
        na = coef * qa + hat[128:256, cols] * back[2, :, cols]
        grad[0:128, cols] = na
        gax[x, 0, :, cols] = jnp.sum(na, axis=0, keepdims=True)
        gax[x, 1, :, cols] = jnp.sum(na * ha, axis=0, keepdims=True)
        gax[x, 2, :, cols] = jnp.sum(qa * ha, axis=0, keepdims=True)
        return carry

    def over_x(buf, s_sem, r_sem):
        return {d: send(buf.at[x], buf.at[x], s_sem.at[d - 1], r_sem.at[d - 1], xdev[d]) for d in NEAR_4}

    def over_z(copies, xbuf, buf, s_sem, r_sem, rows):
        for d in NEAR_4:
            copies[d].wait_recv()
        for i in range(rows):
            buf[z, i] = (xbuf[0, i] + xbuf[1, i]) + (xbuf[2, i] + xbuf[3, i])
        return {d: send(buf.at[z], buf.at[z], s_sem.at[d - 1], r_sem.at[d - 1], zdev[d]) for d in NEAR_Z}

    lax.fori_loop(0, 4, gradient_b, 0)
    bx = over_x(gbx, gbx_s, gbx_r)
    za_forward()
    bz = over_z(bx, gbx, gbz, gbz_s, gbz_r, 2)
    za_finish()
    lax.fori_loop(0, 4, gradient_a, 0)
    ax = over_x(gax, gax_s, gax_r)
    az = over_z(ax, gax, gaz, gaz_s, gaz_r, 3)

    def standard(copies, buf, rows, rstd):
        for d in NEAR_Z:
            copies[d].wait_recv()
        first = sum(buf[k, 0] for k in range(NZ)) * (1.0 / images)
        second = sum(buf[k, 1] for k in range(NZ)) * (1.0 / images)
        hr[rows, :] = (rstd * (grad[rows, :] - first - hat[rows, :] * second)).astype(BF16)

    arows, brows = pl.ds(0, 128), pl.ds(128, 128)
    standard(bz, gbz, brows, rstd_b)
    ob_finish = feat_scatter(
        lambda i: dot_nt(hr[brows, :], rows_of_p(i)), pcs, pcr, pys, pyr, pc_s, pc_r, py_s, py_r
    )
    standard(az, gaz, arows, rstd_a)
    frob = jnp.sum(sum(gaz[k, 2] for k in range(NZ)), axis=1, keepdims=True)
    lo[...] = jnp.broadcast_to(diag + (LAMBDA / (images * images)) * frob, (8, 128))
    lc = send(lo, lorc, lo_s.at[0], lo_r.at[0], cdev)
    oa_finish = feat_scatter(
        lambda i: dot_nt(hr[arows, :], rows_of_p(i)), ocs, ocr, oys, oyr, oc_s, oc_r, oy_s, oy_r
    )
    lc.wait_recv()
    pair = lo[...] + lorc[...]
    lo2[...] = pair
    lly = {d: send(lo2, lory.at[y], lo_s.at[d], lo_r.at[d], ydev[d]) for d in NEAR_4}
    lory[y] = pair
    grads_ref[128:256, :] = ob_finish().astype(BF16)
    grads_ref[0:128, :] = oa_finish().astype(BF16)
    for d in NEAR_4:
        lly[d].wait_recv()
    loss_ref[...] = (lory[0] + lory[1]) + (lory[2] + lory[3])
    for d in NEAR_4:
        za_copy(d - 1, ys[d]).wait_send()
    for cp in sent:
        cp.wait_send()


def on_device(view_a, view_b, projection):
    dma = pltpu.SemaphoreType.DMA
    vmem = pltpu.VMEM
    scratch = [
        vmem((256, 2048), BF16), vmem((2048, 1024), BF16), vmem((256, 1024), F32),
        vmem((256, 1024), BF16), vmem((256, 1024), F32), vmem((3, 1, 1024), F32),
        vmem((2, 4, 128, 256), BF16), vmem((4, 128, 256), BF16), vmem((2, 256, 256), BF16),
        vmem((7, 2, 32, 256), BF16), vmem((8, 256, 256), BF16),
        vmem((8, 3, 1, 256), F32), vmem((2, 256, 256), F32),
        vmem((4, 5, 1, 1024), F32), vmem((8, 5, 1, 1024), F32),
        vmem((4, 256, 256), BF16), vmem((4, 256, 256), BF16), vmem((3, 256, 256), BF16),
        vmem((3, 256, 256), BF16), vmem((8, 128, 256), BF16), vmem((128, 256), BF16),
        vmem((4, 128, 256), BF16), vmem((4, 128, 256), BF16), vmem((3, 128, 256), BF16),
        vmem((3, 128, 256), BF16), vmem((128, 256), F32), vmem((8, 256, 256), BF16),
        vmem((4, 3, 1, 1024), F32), vmem((8, 3, 1, 1024), F32),
        vmem((4, 2, 1, 1024), F32), vmem((8, 2, 1, 1024), F32),
        vmem((4, 128, 256), BF16), vmem((4, 128, 256), BF16), vmem((3, 128, 256), BF16),
        vmem((3, 128, 256), BF16),
        vmem((4, 128, 256), BF16), vmem((4, 128, 256), BF16), vmem((3, 128, 256), BF16),
        vmem((3, 128, 256), BF16),
        vmem((8, 128), F32), vmem((8, 128), F32), vmem((8, 128), F32), vmem((4, 8, 128), F32),
        dma((3,)),
    ]
    sizes = [
        (3,), (3,), (3,), (7, 2), (7,), (7,), (8, 3),
        (3,), (7,), (4,), (3,), (3,), (4,),
        (4,), (3,), (3,), (4,), (3,), (4,),
        (3,), (7,), (3,), (7,), (4,), (3,), (4,), (3,), (4,),
    ]
    for s in sizes:
        scratch += [dma(s), dma(s)]
    loss, grads = pl.pallas_call(
        kernel,
        out_shape=(
            jax.ShapeDtypeStruct((8, 128), F32),
            jax.ShapeDtypeStruct((256, 256), BF16),
        ),
        in_specs=[pl.BlockSpec(memory_space=pltpu.HBM)] * 3,
        out_specs=[pl.BlockSpec(memory_space=pltpu.VMEM)] * 2,
        scratch_shapes=scratch,
        compiler_params=pltpu.CompilerParams(
            collective_id=0, has_side_effects=True, vmem_limit_bytes=54784 * 1024
        ),
        cost_estimate=pl.CostEstimate(flops=5 * 10**9, bytes_accessed=6 * 10**6, transcendentals=0),
        name="twins",
    )(view_a, view_b, projection)
    return loss[0, 0], grads[0:128], grads[128:256]


def solution(mesh):
    in_specs = (P("img", None), P("img", None), P(None, "feat"))
    out_specs = (P(), P("img", "feat"), P("img", "feat"))
    return jax.shard_map(
        on_device, mesh=mesh, in_specs=in_specs, out_specs=out_specs, check_vma=False
    )
```

```python
import functools
import jax
import jax.numpy as jnp
from jax import lax
from jax.experimental import pallas as pl
from jax.experimental.pallas import tpu as pltpu
from jax.sharding import PartitionSpec as P

LAMBDA = 0.0051
EPSILON = 1e-05
MESH = pl.DeviceIdType.MESH
NZ, NX, NY = 8, 4, 4
F32, BF16 = jnp.float32, jnp.bfloat16
NEAR_Z = (1, 7, 2, 6, 3, 5, 4)
NEAR_4 = (1, 3, 2)


def remote(src, dst, send_sem, recv_sem, device):
    return pltpu.make_async_remote_copy(
        src_ref=src, dst_ref=dst, send_sem=send_sem, recv_sem=recv_sem,
        device_id=device, device_id_type=MESH,
    )


def dot_nt(a, b):
    return lax.dot_general(a, b, (((1,), (1,)), ((), ())), preferred_element_type=F32)


def dot_nn(a, b):
    return jnp.dot(a, b, preferred_element_type=F32)


def merge(parts, count):
    n = len(parts)
    ma = sum(p[0] for p in parts) * (1.0 / n)
    mb = sum(p[1] for p in parts) * (1.0 / n)
    da = [p[0] - ma for p in parts]
    db = [p[1] - mb for p in parts]
    saa = sum(p[2] for p in parts) + count * sum(d * d for d in da)
    sbb = sum(p[3] for p in parts) + count * sum(d * d for d in db)
    sab = sum(p[4] for p in parts) + count * sum(d * e for d, e in zip(da, db))
    return [ma, mb, saa, sbb, sab]


def kernel(
    va, vb, proj, loss_ref, grads_ref,
    vv, pw, hat, hr, grad, back,
    xa, xb, tp, tzr, tfull, mz, mcorr,
    stx, stz, lcs, lcr, lys, lyr, la, lb,
    zcs, zcr, zys, zyr, zown, zall, gax, gaz, gbx, gbz,
    ocs, ocr, oys, oyr, pcs, pcr, pys, pyr, lo, lorc, lo2, lory,
    in_sem, xa_s, xa_r, xb_s, xb_r, xc_s, xc_r, tz_s, tz_r, mz_s, mz_r, az_s, az_r, ax_s, ax_r,
    sx_s, sx_r, sz_s, sz_r, lc_s, lc_r, ly_s, ly_r, lay_s, lay_r, lac_s, lac_r,
    zc_s, zc_r, zy_s, zy_r, zay_s, zay_r, zac_s, zac_r, zby_s, zby_r, zbc_s, zbc_r,
    gax_s, gax_r, gaz_s, gaz_r, gbx_s, gbx_r, gbz_s, gbz_r, oc_s, oc_r, oy_s, oy_r, pc_s, pc_r, py_s, py_r, lo_s, lo_r,
):
    images = 128 * NZ * NX
    img, feat = lax.axis_index("img"), lax.axis_index("feat")
    z, x = lax.div(img, NX), lax.rem(img, NX)
    y, core = lax.div(feat, 2), lax.rem(feat, 2)
    zs = [lax.rem(z + d, NZ) for d in range(NZ)]
    xs = [lax.rem(x + d, NX) for d in range(NX)]
    ys = [lax.rem(y + d, NY) for d in range(NY)]
    xback = [lax.rem(x + NX - d, NX) for d in range(NX)]
    yback = [lax.rem(y + NY - d, NY) for d in range(NY)]
    zback = [lax.rem(z + NZ - d, NZ) for d in range(NZ)]
    zdev = [(v * NX + x, feat) for v in zs]
    xdev = [(z * NX + v, feat) for v in xs]
    ydev = [(img, v * 2 + core) for v in ys]
    cdev = (img, y * 2 + 1 - core)

    loads = [
        pltpu.make_async_copy(va, vv.at[pl.ds(0, 128)], in_sem.at[0]),
        pltpu.make_async_copy(vb, vv.at[pl.ds(128, 128)], in_sem.at[1]),
        pltpu.make_async_copy(proj, pw, in_sem.at[2]),
    ]
    for cp in loads:
        cp.start()
    barrier = pltpu.get_barrier_semaphore()
    peers = zdev[1:] + xdev[1:] + ydev[1:] + [cdev]
    for peer in peers:
        pl.semaphore_signal(barrier, inc=1, device_id=peer, device_id_type=MESH)

    sent = []

    def send(src, dst, send_sem, recv_sem, device):
        cp = remote(src, dst, send_sem, recv_sem, device)
        cp.start()
        sent.append(cp)
        return cp

    def cols256(i):
        return pl.ds(pl.multiple_of(i * 256, 256), 256)

    pl.semaphore_wait(barrier, len(peers))
    xac, xbc, xcc = {}, {}, {}
    for d in (2, 1, 3):
        xac[d] = send(
            va.at[:, cols256(xs[d] * 2 + core)], xa.at[core, x],
            xa_s.at[d - 1], xa_r.at[d - 1], xdev[d],
        )
        xbc[d] = send(
            vb.at[:, cols256(feat)], xb.at[x],
            xb_s.at[d - 1], xb_r.at[d - 1], xdev[d],
        )

    loads[0].wait()
    loads[1].wait()
    xa[0, x] = vv[0:128, cols256(x * 2)]
    xa[1, x] = vv[0:128, cols256(x * 2 + 1)]
    xb[x] = vv[128:256, cols256(feat)]

    loads[2].wait()

    def project(n, carry):
        cols = pl.ds(pl.multiple_of(n * 256, 256), 256)
        pr = dot_nn(vv[...], pw[:, cols])
        hat[:, cols] = pr
        pa, pb = pr[0:128], pr[128:256]
        ma = jnp.sum(pa, axis=0, keepdims=True) * (1.0 / 128)
        mb = jnp.sum(pb, axis=0, keepdims=True) * (1.0 / 128)
        pa, pb = pa - ma, pb - mb
        stx[x, 0, :, cols] = ma
        stx[x, 1, :, cols] = mb
        stx[x, 2, :, cols] = jnp.sum(pa * pa, axis=0, keepdims=True)
        stx[x, 3, :, cols] = jnp.sum(pb * pb, axis=0, keepdims=True)
        stx[x, 4, :, cols] = jnp.sum(pa * pb, axis=0, keepdims=True)
        return carry

    lax.fori_loop(0, 4, project, 0)
    sx = {d: send(stx.at[x], stx.at[x], sx_s.at[d - 1], sx_r.at[d - 1], xdev[d]) for d in NEAR_4}

    for d in NEAR_4:
        xac[d].wait_recv()
        there = xa.at[core, xback[d]]
        xcc[d] = send(there, there, xc_s.at[d - 1], xc_r.at[d - 1], cdev)
    for d in NEAR_4:
        sx[d].wait_recv()
    merged = merge([[stx[k, i] for i in range(5)] for k in range(NX)], 128.0)
    for i in range(5):
        stz[z, i] = merged[i]
    sz = {d: send(stz.at[z], stz.at[z], sz_s.at[d - 1], sz_r.at[d - 1], zdev[d]) for d in NEAR_Z}

    for d in NEAR_4:
        xbc[d].wait_recv()
    bcols = xb[...].reshape(512, 256).astype(F32)
    bmean = jnp.sum(bcols, axis=0, keepdims=True) * (1.0 / 512)
    ct = (bcols - bmean).T.astype(BF16)
    mz[z, 2] = bmean
    mzc, tz = {}, {}
    for i, h in enumerate((core, 1 - core)):
        if i == 1:
            for d in NEAR_4:
                xcc[d].wait_recv()
        acols = xa[h].reshape(512, 256).astype(F32)
        amean = jnp.sum(acols, axis=0, keepdims=True) * (1.0 / 512)
        mz[z, h] = amean
        tp[h] = dot_nn(ct, (acols - amean).astype(BF16)).astype(BF16)
        for d in NEAR_Z:
            tz[d, i] = send(
                tp.at[h, pl.ds(pl.multiple_of(zs[d] * 32, 32), 32), :], tzr.at[d - 1, h],
                tz_s.at[d - 1, i], tz_r.at[d - 1, i], zdev[d],
            )
    for d in NEAR_Z:
        mzc[d] = send(mz.at[z], mz.at[z], mz_s.at[d - 1], mz_r.at[d - 1], zdev[d])

    for d in NEAR_Z:
        sz[d].wait_recv()
    mean_a, mean_b, saa, sbb, sab = merge(
        [[stz[k, i] for i in range(5)] for k in range(NZ)], 128.0 * NX
    )
    rstd_a = lax.rsqrt(saa * (1.0 / images) + EPSILON)
    rstd_b = lax.rsqrt(sbb * (1.0 / images) + EPSILON)
    corr = sab * rstd_a * rstd_b * (1.0 / images)
    factor = -2.0 * (1.0 - corr) - 2.0 * LAMBDA * corr
    coef = 2.0 * LAMBDA / images
    diag = jnp.sum((1.0 - corr) ** 2 - LAMBDA * corr * corr, axis=1, keepdims=True)
    hat_a = (hat[0:128, :] - mean_a) * rstd_a
    hat[0:128, :] = hat_a
    hr[0:128, :] = (hat_a * rstd_a).astype(BF16)
    hat_b = (hat[128:256, :] - mean_b) * rstd_b
    hat[128:256, :] = hat_b
    hr[128:256, :] = (hat_b * rstd_b).astype(BF16)

    def feat_scatter(chunk, cs, cr, y_send, y_recv, cs_s, cs_r, ysem_s, ysem_r, between=None):
        cc, yc = {}, {}

        def other(d):
            cs[d] = chunk(ys[d] * 2 + 1 - core).astype(BF16)
            cc[d] = send(cs.at[d], cr.at[d], cs_s.at[d], cs_r.at[d], cdev)

        def own(d):
            mine = chunk(ys[d] * 2 + core)
            cc[d].wait_recv()
            y_send[d - 1] = (mine + cr[d].astype(F32)).astype(BF16)
            yc[d] = send(y_send.at[d - 1], y_recv.at[d - 1], ysem_s.at[d - 1], ysem_r.at[d - 1], ydev[d])

        other(2)
        other(1)
        other(3)
        other(0)
        if between is not None:
            between()
        own(2)
        own(1)
        own(3)
        total = chunk(feat)
        cc[0].wait_recv()
        total = total + cr[0].astype(F32)

        def finish():
            out = total
            for d in NEAR_4:
                yc[d].wait_recv()
                out = out + y_recv[d - 1].astype(F32)
            return out

        return finish

    def feat_gather(at, y_s, y_r, c_s, c_r):
        yc = {d: send(at(feat), at(feat), y_s.at[d - 1], y_r.at[d - 1], ydev[d]) for d in NEAR_4}
        cc = {0: send(at(feat), at(feat), c_s.at[0], c_r.at[0], cdev)}

        def forward():
            for d in NEAR_4:
                yc[d].wait_recv()
                there = at(yback[d] * 2 + core)
                cc[d] = send(there, there, c_s.at[d], c_r.at[d], cdev)

        def finish():
            for d in range(4):
                cc[d].wait_recv()

        return forward, finish

    def rows_of_p(i):
        return pw[pl.ds(pl.multiple_of(i * 256, 256), 256), :]

    l_finish = feat_scatter(
        lambda i: dot_nt(hr[...], rows_of_p(i)), lcs, lcr, lys, lyr, lc_s, lc_r, ly_s, ly_r
    )
    for d in NEAR_Z:
        mzc[d].wait_recv()
    am = [jnp.concatenate([mz[k, i] for k in range(NZ)], axis=0) for i in range(3)]
    am = [m - jnp.sum(m, axis=0, keepdims=True) * (1.0 / NZ) for m in am]
    bm = (am[2] * 512.0).T.astype(BF16)
    zrows = pl.ds(pl.multiple_of(z * 32, 32), 32)
    for h in range(2):
        mcorr[h] = dot_nn(bm, am[h].astype(BF16))
    total = tp[:, zrows, :].astype(F32) + mcorr[:, zrows, :]
    for d in NEAR_Z:
        tz[d, 0].wait_recv()
        tz[d, 1].wait_recv()
        total = total + tzr[d - 1].astype(F32)
    tfull[pl.ds(2 * x, 2), zrows, :] = total.astype(BF16)
    mine = tfull.at[pl.ds(2 * x, 2), zrows, :]
    az = {d: send(mine, mine, az_s.at[d - 1], az_r.at[d - 1], zdev[d]) for d in NEAR_Z}
    ax = {}
    for e in NEAR_4:
        ax[0, e] = send(mine, mine, ax_s.at[0, e - 1], ax_r.at[0, e - 1], xdev[e])

    def piece(d, e):
        there = tfull.at[pl.ds(2 * x, 2), pl.ds(pl.multiple_of(zback[d] * 32, 32), 32), :]
        ax[d, e] = send(there, there, ax_s.at[d, e - 1], ax_r.at[d, e - 1], xdev[e])

    def forward(zset):
        for d in zset:
            az[d].wait_recv()
            for e in NEAR_4:
                piece(d, e)

    forward((1, 7, 2, 6))
    total = l_finish()
    la[feat] = total[0:128].astype(BF16)
    lb[...] = total[128:256].astype(BF16)
    la_forward, la_finish = feat_gather(lambda i: la.at[i], lay_s, lay_r, lac_s, lac_r)
    forward((3, 5, 4))

    zcc = {}

    def za_other(e):
        zcs[e] = dot_nn(lb[...], tfull[xback[e] * 2 + 1 - core]).astype(BF16)
        zcc[e] = send(zcs.at[e], zcr.at[e], zc_s.at[e], zc_r.at[e], cdev)

    def za_copy(slot, there):
        return remote(
            zys.at[slot], zyr.at[slot], zy_s.at[slot], zy_r.at[slot], (img, there * 2 + core)
        )

    def za_own(e):
        there = xback[e]
        total = dot_nn(lb[...], tfull[there * 2 + core])
        zcc[e].wait_recv()
        total = total + zcr[e].astype(F32)
        slot = jnp.maximum(lax.rem(there - y + NY, NY) - 1, 0)

        @pl.when(there == y)
        def _():
            zown[...] = total

        @pl.when(there != y)
        def _():
            zys[slot] = total.astype(BF16)
            za_copy(slot, there).start()

    def zb_part(e):
        i = xback[e] * 2
        return dot_nt(la[i], tfull[i]) + dot_nt(la[i + 1], tfull[i + 1])

    def quarter(e):
        for d in (0,) + NEAR_Z:
            ax[d, e].wait_recv()

    za_other(0)
    la_forward()
    za_own(0)
    quarter(1)
    za_other(1)
    la_finish()
    zb = zb_part(0)
    za_own(1)
    quarter(3)
    za_other(3)
    zb = zb + zb_part(1)
    za_own(3)
    zb = zb + zb_part(3)
    quarter(2)
    za_other(2)
    zb = zb + zb_part(2)
    za_own(2)
    zall[feat, 128:256, :] = zb.astype(BF16)
    zb_forward, zb_finish = feat_gather(
        lambda i: zall.at[i, pl.ds(128, 128), :], zby_s, zby_r, zbc_s, zbc_r
    )
    for d in NEAR_4:
        za_copy(d - 1, ys[d]).wait_recv()
    total = zown[...] + zyr[0].astype(F32) + zyr[1].astype(F32) + zyr[2].astype(F32)
    zall[feat, 0:128, :] = total.astype(BF16)
    za_forward, za_finish = feat_gather(
        lambda i: zall.at[i, pl.ds(0, 128), :], zay_s, zay_r, zac_s, zac_r
    )
    zb_forward()
    zb_finish()

    back[0] = rstd_a
    back[1] = rstd_b
    back[2] = factor

    def gradient_b(n, carry):
        cols = cols256(n)
        g = sum(dot_nn(zall[i, 128:256, :], pw[i * 256:(i + 1) * 256, cols]) for i in range(8))
        hb = hat[128:256, cols]
        nb = coef * (g * back[1, :, cols]) + hat[0:128, cols] * back[2, :, cols]
        grad[128:256, cols] = nb
        gbx[x, 0, :, cols] = jnp.sum(nb, axis=0, keepdims=True)
        gbx[x, 1, :, cols] = jnp.sum(nb * hb, axis=0, keepdims=True)
        return carry

    def gradient_a(n, carry):
        cols = cols256(n)
        g = sum(dot_nn(zall[i, 0:128, :], pw[i * 256:(i + 1) * 256, cols]) for i in range(8))
        ha = hat[0:128, cols]
        qa = g * back[0, :, cols]
        na = coef * qa + hat[128:256, cols] * back[2, :, cols]
        grad[0:128, cols] = na
        gax[x, 0, :, cols] = jnp.sum(na, axis=0, keepdims=True)
        gax[x, 1, :, cols] = jnp.sum(na * ha, axis=0, keepdims=True)
        gax[x, 2, :, cols] = jnp.sum(qa * ha, axis=0, keepdims=True)
        return carry

    def over_x(buf, s_sem, r_sem):
        return {d: send(buf.at[x], buf.at[x], s_sem.at[d - 1], r_sem.at[d - 1], xdev[d]) for d in NEAR_4}

    def over_z(copies, xbuf, buf, s_sem, r_sem, rows):
        for d in NEAR_4:
            copies[d].wait_recv()
        for i in range(rows):
            buf[z, i] = (xbuf[0, i] + xbuf[1, i]) + (xbuf[2, i] + xbuf[3, i])
        return {d: send(buf.at[z], buf.at[z], s_sem.at[d - 1], r_sem.at[d - 1], zdev[d]) for d in NEAR_Z}

    lax.fori_loop(0, 4, gradient_b, 0)
    bx = over_x(gbx, gbx_s, gbx_r)
    za_forward()
    bz = over_z(bx, gbx, gbz, gbz_s, gbz_r, 2)
    za_finish()
    lax.fori_loop(0, 4, gradient_a, 0)
    ax = over_x(gax, gax_s, gax_r)
    az = over_z(ax, gax, gaz, gaz_s, gaz_r, 3)

    def standard(copies, buf, rows, rstd):
        for d in NEAR_Z:
            copies[d].wait_recv()
        first = sum(buf[k, 0] for k in range(NZ)) * (1.0 / images)
        second = sum(buf[k, 1] for k in range(NZ)) * (1.0 / images)
        hr[rows, :] = (rstd * (grad[rows, :] - first - hat[rows, :] * second)).astype(BF16)

    arows, brows = pl.ds(0, 128), pl.ds(128, 128)
    standard(bz, gbz, brows, rstd_b)
    ob_finish = feat_scatter(
        lambda i: dot_nt(hr[brows, :], rows_of_p(i)), pcs, pcr, pys, pyr, pc_s, pc_r, py_s, py_r
    )
    standard(az, gaz, arows, rstd_a)
    frob = jnp.sum(sum(gaz[k, 2] for k in range(NZ)), axis=1, keepdims=True)
    lo[...] = jnp.broadcast_to(diag + (LAMBDA / (images * images)) * frob, (8, 128))
    lc = send(lo, lorc, lo_s.at[0], lo_r.at[0], cdev)
    lly = {}

    def loss_over_y():
        lc.wait_recv()
        pair = lo[...] + lorc[...]
        lo2[...] = pair
        for d in NEAR_4:
            lly[d] = send(lo2, lory.at[y], lo_s.at[d], lo_r.at[d], ydev[d])
        lory[y] = pair

    oa_finish = feat_scatter(
        lambda i: dot_nt(hr[arows, :], rows_of_p(i)), ocs, ocr, oys, oyr, oc_s, oc_r, oy_s, oy_r,
        loss_over_y,
    )
    grads_ref[128:256, :] = ob_finish().astype(BF16)
    grads_ref[0:128, :] = oa_finish().astype(BF16)
    for d in NEAR_4:
        lly[d].wait_recv()
    loss_ref[...] = (lory[0] + lory[1]) + (lory[2] + lory[3])
    for d in NEAR_4:
        za_copy(d - 1, ys[d]).wait_send()
    for cp in sent:
        cp.wait_send()


def on_device(view_a, view_b, projection):
    dma = pltpu.SemaphoreType.DMA
    vmem = pltpu.VMEM
    scratch = [
        vmem((256, 2048), BF16), vmem((2048, 1024), BF16), vmem((256, 1024), F32),
        vmem((256, 1024), BF16), vmem((256, 1024), F32), vmem((3, 1, 1024), F32),
        vmem((2, 4, 128, 256), BF16), vmem((4, 128, 256), BF16), vmem((2, 256, 256), BF16),
        vmem((7, 2, 32, 256), BF16), vmem((8, 256, 256), BF16),
        vmem((8, 3, 1, 256), F32), vmem((2, 256, 256), F32),
        vmem((4, 5, 1, 1024), F32), vmem((8, 5, 1, 1024), F32),
        vmem((4, 256, 256), BF16), vmem((4, 256, 256), BF16), vmem((3, 256, 256), BF16),
        vmem((3, 256, 256), BF16), vmem((8, 128, 256), BF16), vmem((128, 256), BF16),
        vmem((4, 128, 256), BF16), vmem((4, 128, 256), BF16), vmem((3, 128, 256), BF16),
        vmem((3, 128, 256), BF16), vmem((128, 256), F32), vmem((8, 256, 256), BF16),
        vmem((4, 3, 1, 1024), F32), vmem((8, 3, 1, 1024), F32),
        vmem((4, 2, 1, 1024), F32), vmem((8, 2, 1, 1024), F32),
        vmem((4, 128, 256), BF16), vmem((4, 128, 256), BF16), vmem((3, 128, 256), BF16),
        vmem((3, 128, 256), BF16),
        vmem((4, 128, 256), BF16), vmem((4, 128, 256), BF16), vmem((3, 128, 256), BF16),
        vmem((3, 128, 256), BF16),
        vmem((8, 128), F32), vmem((8, 128), F32), vmem((8, 128), F32), vmem((4, 8, 128), F32),
        dma((3,)),
    ]
    sizes = [
        (3,), (3,), (3,), (7, 2), (7,), (7,), (8, 3),
        (3,), (7,), (4,), (3,), (3,), (4,),
        (4,), (3,), (3,), (4,), (3,), (4,),
        (3,), (7,), (3,), (7,), (4,), (3,), (4,), (3,), (4,),
    ]
    for s in sizes:
        scratch += [dma(s), dma(s)]
    loss, grads = pl.pallas_call(
        kernel,
        out_shape=(
            jax.ShapeDtypeStruct((8, 128), F32),
            jax.ShapeDtypeStruct((256, 256), BF16),
        ),
        in_specs=[pl.BlockSpec(memory_space=pltpu.HBM)] * 3,
        out_specs=[pl.BlockSpec(memory_space=pltpu.VMEM)] * 2,
        scratch_shapes=scratch,
        compiler_params=pltpu.CompilerParams(
            collective_id=0, has_side_effects=True, vmem_limit_bytes=54784 * 1024
        ),
        cost_estimate=pl.CostEstimate(flops=5 * 10**9, bytes_accessed=6 * 10**6, transcendentals=0),
        name="twins",
    )(view_a, view_b, projection)
    return loss[0, 0], grads[0:128], grads[128:256]


def solution(mesh):
    in_specs = (P("img", None), P("img", None), P(None, "feat"))
    out_specs = (P(), P("img", "feat"), P("img", "feat"))
    return jax.shard_map(
        on_device, mesh=mesh, in_specs=in_specs, out_specs=out_specs, check_vma=False
    )
```
